256 devices in a mesh: shower: 8 (over x, core), seq: 32 (over y, z).
Axes of the slice: x: 4, y: 4, z: 8, core: 2. Of those that a mesh axis runs over, the one named last changes fastest.
Arguments:
- ssm_input: bfloat16 [8, 8192, 2048], P('shower', 'seq'), may hold values from -6 to 6
- gate_input: bfloat16 [8, 8192, 2048], P('shower', 'seq'), may hold values from -6 to 6
- state_input: bfloat16 [8, 8192, 128], P('shower', 'seq'), may hold values from -6 to 6
- state_output: bfloat16 [8, 8192, 128], P('shower', 'seq'), may hold values from -0.52734375 to 0.52734375
- log_decay: float32 [8, 8192, 16], P('shower', 'seq'), may hold values from -1 to 0, as said below
- norm_gain: float32 [2048], replicated, may hold values from 0.1 to 1.9
- out_weight: bfloat16 [1024, 2048], P(None, ('shower', 'seq')), may hold values from -0.125 to 0.125
- grad_output: bfloat16 [8, 8192, 1024], P('shower', 'seq'), may hold values from -6 to 6
Outputs:
- grad_input: bfloat16 [8, 8192, 2048], P('shower', 'seq')
- grad_gate: bfloat16 [8, 8192, 2048], P('shower', 'seq')
- grad_state_in: bfloat16 [8, 8192, 128], P('shower', 'seq')
- grad_state_out: bfloat16 [8, 8192, 128], P('shower', 'seq')
- grad_log_decay: float32 [8, 8192, 16], P('shower', 'seq')
- grad_out_weight: float32 [1024, 2048], P(('shower', 'seq'))
- grad_norm_gain: float32 [2048], P(('shower', 'seq'))
The draws below stay inside these ranges and needn't reach their ends.
Inputs may be any that keep to these rules, and one draw needn't show every extreme that they name: `log_decay`: negative per-step log decays.
All inputs are finite; a program needn't handle non-finite values.
Results may differ from the reference program's by a relative error of at most 0.022.
Values may be sent and summed in bfloat16 or wider, within the bound.
No kernel may reach another device: no remote copies, remote signals or barrier semaphores. Data moves between devices by JAX's collectives and lax.ppermute only.
A program may use at most 128 MiB of HBM per device.

```python
import math
import jax
import jax.numpy as jnp
from jax import lax

D = 1024
H = 16
P_SIZE = 128
N = 128
GROUP = 256
TOK_DEV = 256
INNER = 2048
LENGTH = 8192
SHOWERS = 8


def draw_log_decay(key, part):
    sampler_seeds = jax.random.split(key, 9)
    tensor_dimensions = (SHOWERS, LENGTH, H)
    pick = jax.random.uniform(sampler_seeds[0], (SHOWERS, 1, H))
    quick = pick < 0.25
    middle = (pick >= 0.25) & (pick < 0.5)
    quick_rate = jax.random.uniform(sampler_seeds[1], (SHOWERS, 1, H), minval=1.0 / 50.0, maxval=1.0 / 30.0)
    middle_rate = jnp.exp(jax.random.uniform(sampler_seeds[2], (SHOWERS, 1, H), minval=math.log(1.0 / 1000.0), maxval=math.log(1.0 / 250.0)))
    slow_rate = jnp.exp(jax.random.uniform(sampler_seeds[3], (SHOWERS, 1, H), minval=math.log(0.3), maxval=0.0)) / LENGTH
    reference_decay_speed = jnp.where(quick, quick_rate, jnp.where(middle, middle_rate, slow_rate))
    blocks = LENGTH // TOK_DEV
    segment_factor = jnp.exp(jax.random.uniform(sampler_seeds[4], (SHOWERS, blocks, 1, H), minval=-math.log(2.0), maxval=math.log(2.0)))
    segment_factor = jnp.broadcast_to(segment_factor, (SHOWERS, blocks, TOK_DEV, H)).reshape(tensor_dimensions)
    rough_approximation = jnp.exp(jax.random.uniform(sampler_seeds[5], tensor_dimensions, minval=-math.log(2.0), maxval=math.log(2.0)))
    group_count = LENGTH // GROUP
    which_group = jax.random.randint(sampler_seeds[6], (SHOWERS, 2, H), 0, group_count)
    offset = jax.random.randint(sampler_seeds[7], (SHOWERS, 2, H), GROUP // 4, GROUP - GROUP // 4)
    places = which_group * GROUP + offset
    position = jnp.arange(LENGTH, dtype=jnp.int32)[None, :, None]
    hit_cells = (position == places[:, 0:1, :]) | (position == places[:, 1:2, :])
    cascade_spike = jnp.log(1.0 - jax.random.uniform(sampler_seeds[8], tensor_dimensions, minval=0.2, maxval=0.5))
    scalar_element = -reference_decay_speed * segment_factor * rough_approximation + jnp.where(hit_cells, cascade_spike, 0.0)
    return scalar_element.astype(jnp.float32)


def raised(entries, rng, source, target, parts, factor):
    def block_of(axis_at):
        return (jnp.arange(entries.shape[axis_at]) // (entries.shape[axis_at] // parts)).reshape((-1,) + (1,) * (entries.ndim - 1 - axis_at))

    one_side = jax.random.permutation(rng, parts)[block_of(target)]
    second = (block_of(target) + parts // 2) % parts
    return jnp.where((block_of(source) == one_side) | (block_of(source) == second), factor * entries, entries)


def steps_of(stream_key, shape, cuts, low, top_value):
    def one(dim, blocks):
        steps = jax.random.uniform(jax.random.fold_in(jax.random.fold_in(stream_key, 6), dim), (blocks,), jnp.float32, low / len(cuts), top_value / len(cuts))
        return jnp.repeat(jnp.exp(steps), shape[dim] // blocks).reshape((-1,) + (1,) * (len(shape) - dim - 1))

    gain = one(*cuts[0])
    for cut in cuts[1:]:
        gain = gain * one(*cut)
    return gain


def gaussian(stream_key, dims, spread, limit, cuts=(), held_as=jnp.bfloat16):
    values = jax.random.normal(stream_key, dims, jnp.float32) * spread
    if len(cuts) > 0:
        values = steps_of(stream_key, dims, cuts, -0.22, 0.18) * values
    return jnp.clip(values, min=-limit, max=limit).astype(held_as)


def bell_draw_with(rng, extent, deviation, bound, shards, heavy, held_as=jnp.bfloat16):
    array = deviation * jax.random.normal(rng, extent, jnp.float32)
    if shards:
        array = array * steps_of(rng, extent, shards, -0.22, 0.18)
    return jnp.clip(raised(array, jax.random.fold_in(rng, 3), *heavy), -bound, bound).astype(held_as)


def setup_inputs(seed: int = 0) -> dict:
    key_list = jax.random.split(jax.random.key(seed), 9)
    ssm_input = gaussian(key_list[0], (SHOWERS, LENGTH, INNER), 1.0, 6.0, ((0, 8), (1, 32)))
    gate_input = gaussian(key_list[1], (SHOWERS, LENGTH, INNER), 1.0, 6.0, ((0, 8), (1, 32)))
    state_input = gaussian(key_list[2], (SHOWERS, LENGTH, N), 1.0, 6.0, ((0, 8), (1, 32)))
    state_output = gaussian(key_list[3], (SHOWERS, LENGTH, N), (N ** -0.5), 0.52734375, ((0, 8), (1, 32)))
    log_decay = draw_log_decay(jax.random.fold_in(key_list[8], 71), 0)
    norm_gain = jnp.clip(1.0 + 0.18 * jax.random.normal(key_list[5], (INNER,), jnp.float32), 0.1, 1.9)
    out_weight = gaussian(key_list[6], (D, INNER), INNER ** -0.5, 0.125, ((1, 256),))
    grad_output = bell_draw_with(key_list[7], (SHOWERS, LENGTH, D), 1.0, 6.0, ((0, 8), (1, 32)), (1, 2, 32, 2.75))
    return {"ssm_input": ssm_input, "gate_input": gate_input, "state_input": state_input, "state_output": state_output, "log_decay": log_decay, "norm_gain": norm_gain, "out_weight": out_weight, "grad_output": grad_output}


HIGHEST = lax.Precision.HIGHEST

def rounded(scalar_element):
    return lax.optimization_barrier(scalar_element.astype(jnp.bfloat16)).astype(jnp.float32)

def decay_table(cum_decay):
    along = cum_decay.T
    differ = along[:, :, None] - along[:, None, :]
    row_index = lax.broadcasted_iota(jnp.int32, differ.shape, 1)
    col_index = lax.broadcasted_iota(jnp.int32, differ.shape, 2)
    causal = row_index >= col_index
    return jnp.where(causal, jnp.exp(jnp.where(causal, differ, 0.0)), 0.0)

def group_pieces(x_raw, b_raw, c_raw, cum_decay):
    group_total = cum_decay[-1]
    table = decay_table(cum_decay)
    kernel = rounded(jnp.dot(c_raw, b_raw.T, preferred_element_type=jnp.float32)[None] * table)
    keep_start = jnp.exp(cum_decay)
    keep_end = jnp.exp(group_total[None, :] - cum_decay)
    x_float = x_raw.astype(jnp.float32)
    x_end = rounded(x_float * keep_end[:, :, None])
    return (x_float, table, kernel, keep_start, keep_end, x_end)

def group_forward(state, item):
    x_raw, b_raw, c_raw, cum_decay = item
    x_float, table, kernel, keep_start, keep_end, x_end = group_pieces(x_raw, b_raw, c_raw, cum_decay)
    b_float = b_raw.astype(jnp.float32)
    c_float = c_raw.astype(jnp.float32)
    entering_bf = rounded(state)
    inner_part = jnp.einsum('hts,shp->thp', kernel, x_float, precision=HIGHEST)
    carried = jnp.einsum('hpn,tn->thp', entering_bf, c_float, precision=HIGHEST)
    output_y = inner_part + keep_start[:, :, None] * carried
    group_state = jnp.einsum('shp,sn->hpn', x_end, b_float, precision=HIGHEST)
    next_state = jnp.exp(cum_decay[-1])[:, None, None] * state + group_state
    return (next_state, (output_y, entering_bf))

def group_gradient(state, item):
    grad_block, c_raw, cum_decay = item
    grad_start = rounded(grad_block * jnp.exp(cum_decay)[:, :, None])
    grad_group = jnp.einsum('thp,tn->hpn', grad_start, c_raw.astype(jnp.float32), precision=HIGHEST)
    next_state = jnp.exp(cum_decay[-1])[:, None, None] * state + grad_group
    return (next_state, rounded(state))

def group_backward(item):
    x_raw, b_raw, c_raw, cum_decay, grad_block, entering_bf, leaving_bf, output_y = item
    x_float, table, kernel, keep_start, keep_end, x_end = group_pieces(x_raw, b_raw, c_raw, cum_decay)
    b_float = b_raw.astype(jnp.float32)
    c_float = c_raw.astype(jnp.float32)
    grad_bf = rounded(grad_block)
    grad_start = rounded(grad_block * keep_start[:, :, None])
    grad_xf = jnp.einsum('hts,thp->shp', kernel, grad_bf, precision=HIGHEST)
    grad_xf = grad_xf + keep_end[:, :, None] * jnp.einsum('hpn,sn->shp', leaving_bf, b_float, precision=HIGHEST)
    pair_weights = rounded(jnp.einsum('thp,shp->hts', grad_bf, x_float, precision=HIGHEST) * table)
    grad_c = jnp.einsum('hts,sn->tn', pair_weights, b_float, precision=HIGHEST)
    grad_c = grad_c + jnp.einsum('thp,hpn->tn', grad_start, entering_bf, precision=HIGHEST)
    grad_b = jnp.einsum('hts,tn->sn', pair_weights, c_float, precision=HIGHEST)
    grad_b = grad_b + jnp.einsum('shp,hpn->sn', x_end, leaving_bf, precision=HIGHEST)
    rate_term = lax.optimization_barrier(jnp.sum(grad_block * output_y, axis=-1)) - lax.optimization_barrier(jnp.sum(x_float * grad_xf, axis=-1))
    return (grad_xf, grad_c, grad_b, rate_term)

def norm_backward(output_flat, gate_input, norm_gain, out_weight, grad_output):
    gate_float = gate_input.astype(jnp.float32)
    sigmoid_gate = jax.nn.sigmoid(gate_float)
    active = gate_float * sigmoid_gate
    pre_norm = output_flat * active
    inv_rms = lax.rsqrt(lax.optimization_barrier(jnp.mean(pre_norm * pre_norm, axis=-1, keepdims=True)) + 1e-05)
    normed = (pre_norm * inv_rms * norm_gain).astype(jnp.bfloat16)
    grad_normed = jnp.dot(grad_output, out_weight, preferred_element_type=jnp.float32)
    scaled = norm_gain * grad_normed
    grad_pre = inv_rms * scaled - pre_norm * (inv_rms * inv_rms * inv_rms) * lax.optimization_barrier(jnp.mean(scaled * pre_norm, axis=-1, keepdims=True))
    grad_y = grad_pre * active
    grad_gate = (grad_pre * output_flat * sigmoid_gate * (1.0 + gate_float * (1.0 - sigmoid_gate))).astype(jnp.bfloat16)
    gain_term = lax.optimization_barrier(jnp.sum(grad_normed * pre_norm * inv_rms, axis=0))
    return (grad_y, grad_gate, normed, gain_term)

def shower_grads(ssm_input, gate_input, state_input, state_output, log_decay, grad_output, norm_gain, out_weight):
    groups = LENGTH // GROUP
    x_raw = ssm_input.reshape(groups, GROUP, H, P_SIZE)
    b_raw = state_input.reshape(groups, GROUP, N)
    c_raw = state_output.reshape(groups, GROUP, N)
    cum_decay = jnp.cumsum(log_decay.reshape(groups, GROUP, H), axis=1)
    start_state = jnp.zeros((H, P_SIZE, N), jnp.float32)
    _, (output_y, entering_bf) = lax.scan(group_forward, start_state, (x_raw, b_raw, c_raw, cum_decay))
    grad_y, grad_gate, normed, gain_term = norm_backward(output_y.reshape(LENGTH, H * P_SIZE), gate_input, norm_gain, out_weight, grad_output)
    grad_heads = grad_y.reshape(groups, GROUP, H, P_SIZE)
    _, leaving_bf = lax.scan(group_gradient, start_state, (grad_heads, c_raw, cum_decay), reverse=True)
    grad_xf, grad_c, grad_b, rate_term = lax.map(group_backward, (x_raw, b_raw, c_raw, cum_decay, grad_heads, entering_bf, leaving_bf, output_y))
    rate_flat = rate_term.reshape(LENGTH, H)
    grad_log_decay = jnp.flip(jnp.cumsum(jnp.flip(rate_flat, 0), axis=0), 0)
    weight_term = jnp.einsum('td,ti->di', grad_output, normed, preferred_element_type=jnp.float32)
    return (grad_xf.reshape(LENGTH, H * P_SIZE).astype(jnp.bfloat16), grad_gate, grad_b.reshape(LENGTH, N).astype(jnp.bfloat16), grad_c.reshape(LENGTH, N).astype(jnp.bfloat16), grad_log_decay, weight_term, gain_term)

def reference(ssm_input, gate_input, state_input, state_output, log_decay, norm_gain, out_weight, grad_output):

    def one_shower(item):
        return shower_grads(item[0], item[1], item[2], item[3], item[4], item[5], norm_gain, out_weight)
    results = lax.map(one_shower, (ssm_input, gate_input, state_input, state_output, log_decay, grad_output))
    grad_input, grad_gate, grad_state_in, grad_state_out, grad_log_decay, weight_terms, gain_terms = results
    return (grad_input, grad_gate, grad_state_in, grad_state_out, grad_log_decay, lax.optimization_barrier(jnp.sum(weight_terms, axis=0)), lax.optimization_barrier(jnp.sum(gain_terms, axis=0)))
```

```python
import functools

import jax
import jax.numpy as jnp
from jax import lax
from jax.experimental import pallas as pl
from jax.experimental.pallas import tpu as pltpu
from jax.sharding import Mesh
from jax.sharding import PartitionSpec as P

F32, BF16 = jnp.float32, jnp.bfloat16
T = 256
H = 16
W = 128
INNER = H * W
D = 1024
SEQ = 32
HALF = 64
EXTRA = 16
GAINROWS = 16
SEQ_AXES = ("y", "z")
FAR = -1e30
HI = lax.Precision.HIGHEST


def lane(h, width=W):
    return pl.ds(pl.multiple_of(h * width, width), width)


def dot(a, b, ca=1, cb=0, precision=None):
    return lax.dot_general(
        a, b, (((ca,), (cb,)), ((), ())), precision=precision, preferred_element_type=F32
    )


def iota(shape, axis):
    return lax.broadcasted_iota(jnp.int32, shape, axis)


def row_sum(a):
    return jnp.sum(a, axis=1, keepdims=True)


def pair_cols(ref, h):
    return jnp.concatenate([ref[2 * h], ref[2 * h + 1]], axis=1)


def pair_state(ref, h):
    blocks = ref[pl.ds(4 * h, 4)]
    first = blocks[0:2].reshape(W, W)
    second = blocks[2:4].reshape(W, W)
    return jnp.concatenate([first, second], axis=1)


def split_state(ref, h, value):
    ref[pl.ds(4 * h, 2), 0:HALF, :] = value[:, :W].reshape(2, HALF, W)
    ref[pl.ds(4 * h + 2, 2), 0:HALF, :] = value[:, W:].reshape(2, HALF, W)


def state_kernel(x_ref, b_ref, decay_ref, send_ref, state_ref, col_ref, row_ref, end_ref):
    tri = (iota((T, T), 0) >= iota((T, T), 1)).astype(F32)
    decay = decay_ref[...]
    cum = dot(tri, decay, precision=HI)
    row_ref[...] = dot(decay, tri, 0, 1, precision=HI)
    for h in range(H):
        col_ref[h] = jnp.broadcast_to(cum[:, h : h + 1], (T, W))
    b = b_ref[...]

    @pl.loop(0, H // 2)
    def _(h):
        col = pair_cols(col_ref, h)
        total = col[T - 1 : T, :]
        cols = lane(h, 2 * W)
        x_end = (x_ref[:, cols].astype(F32) * jnp.exp(total - col)).astype(BF16)
        end_ref[:, cols] = x_end
        state = dot(b, x_end, 0, 0)
        state_ref[:, cols] = state
        split_state(send_ref, h, state.astype(BF16))
        high = total.astype(BF16).astype(F32)
        middle = (total - high).astype(BF16).astype(F32)
        low = total - high - middle
        at = iota((EXTRA, 2 * W), 0)
        rows = jnp.where(at == 0, high, jnp.where(at == 1, middle, jnp.where(at == 2, low, 0.0)))
        rows = rows.astype(BF16)
        for k in range(4):
            half = rows[:, :W] if k < 2 else rows[:, W:]
            send_ref[4 * h + k, HALF : HALF + EXTRA, :] = half


def forward_scan_kernel(got_ref, out_ref, factor_ref):
    def step(j, carry):
        out_ref[j] = carry.astype(BF16)
        tail = got_ref[j, HALF : HALF + EXTRA, :].astype(F32)
        factor = jnp.exp(jnp.sum(tail, axis=0, keepdims=True))
        factor_ref[pl.ds(j, 1), :] = factor
        return factor * carry + got_ref[j, 0:HALF, :].astype(F32)

    lax.fori_loop(0, SEQ, step, jnp.zeros((HALF, W), F32))


def backward_scan_kernel(got_ref, factor_ref, out_ref):
    def step(k, carry):
        j = SEQ - 1 - k
        out_ref[j] = carry.astype(BF16)
        return factor_ref[pl.ds(j, 1), :] * carry + got_ref[j].astype(F32)

    lax.fori_loop(0, SEQ, step, jnp.zeros((HALF, W), F32))


def inner_kernel(x_ref, b_ref, c_ref, col_ref, row_ref, inner_ref):
    scores = dot(c_ref[...], b_ref[...], 1, 1)
    causal = iota((T, T), 0) >= iota((T, T), 1)

    @pl.loop(0, H)
    def _(h):
        col = col_ref[h]
        differ = jnp.concatenate([col, col], axis=1) - row_ref[pl.ds(h, 1), :]
        kernel = (scores * jnp.exp(jnp.where(causal, differ, FAR))).astype(BF16)
        inner_ref[:, lane(h)] = dot(kernel, x_ref[:, lane(h)])


def normed_grad_kernel(at_ref, grad_ref, *refs):
    *pieces, out_ref = refs
    grad = grad_ref[...]
    x, c = at_ref[0], at_ref[1]
    for core in range(2):
        for k in range(4):
            source = lax.rem(x + 4 - k, 4) * 2 + (c if core == 0 else 1 - c)
            out_ref[:, lane(source, 2 * W)] = dot(grad, pieces[core * 4 + k][...], 1, 1)


def norm_kernel(
    inner_ref, gn_ref, gate_ref, enter_ref, c_ref, col_ref, gain_ref,
    gate_out, grad_out, start_out, normed_out, send_ref, gain_out, rate_out, y_ref, u_ref,
):
    c = c_ref[...]

    def first(h, sums):
        squares, mixed = sums
        cols = lane(h, 2 * W)
        keep = jnp.exp(pair_cols(col_ref, h))
        y = inner_ref[:, cols] + keep * dot(c, pair_state(enter_ref, h))
        gate = gate_ref[:, cols].astype(F32)
        u = y * (gate * jax.nn.sigmoid(gate))
        y_ref[:, cols] = y
        u_ref[:, cols] = u
        both = gain_ref[:, cols] * gn_ref[:, cols] * u
        squared = u * u
        return (
            squares + squared[:, :W] + squared[:, W:],
            mixed + both[:, :W] + both[:, W:],
        )

    zero = jnp.zeros((T, W), F32)
    squares, mixed = lax.fori_loop(0, H // 2, first, (zero, zero))
    rstd = lax.rsqrt(row_sum(squares) / INNER + 1e-5)
    pull = rstd * rstd * rstd * (row_sum(mixed) / INNER)
    rate_out[...] = zero

    @pl.loop(0, H // 2)
    def _(h):
        cols = lane(h, 2 * W)
        y, u, gn = y_ref[:, cols], u_ref[:, cols], gn_ref[:, cols]
        gain = gain_ref[:, cols]
        gate = gate_ref[:, cols].astype(F32)
        sig = jax.nn.sigmoid(gate)
        normal = u * rstd
        grad_u = rstd * (gain * gn) - u * pull
        grad_y = grad_u * (gate * sig)
        gate_out[:, cols] = (grad_u * y * sig * (1.0 + gate * (1.0 - sig))).astype(BF16)
        normed_out[:, cols] = (normal * gain).astype(BF16)
        gain_out[:, cols] = jnp.sum(gn * normal, axis=0, keepdims=True)
        grad_out[:, cols] = grad_y.astype(BF16)
        start = (grad_y * jnp.exp(pair_cols(col_ref, h))).astype(BF16)
        start_out[:, cols] = start
        rate = grad_y * y
        at = iota((T, W), 1)
        rates = rate_out[...]
        rates = jnp.where(at == 2 * h, row_sum(rate[:, :W]), rates)
        rate_out[...] = jnp.where(at == 2 * h + 1, row_sum(rate[:, W:]), rates)
        split_state(send_ref, h, dot(c, start, 0, 0).astype(BF16))


def weight_kernel(at_ref, grad_ref, normed_ref, gain_ref, *outs):
    x, c = at_ref[0], at_ref[1]
    normed = normed_ref[...]
    for core in range(2):
        for k in range(4):
            block = lax.rem(x + k, 4) * 2 + (c if core == 0 else 1 - c)
            out = outs[core * 4 + k]
            out[0:W, :] = dot(grad_ref[:, lane(block)], normed, 0, 0).astype(BF16)
            gain = jnp.broadcast_to(gain_ref[:, lane(block, 2 * W)], (GAINROWS, 2 * W))
            out[W : W + GAINROWS, :] = jnp.zeros((GAINROWS, INNER), BF16)
            out[W : W + GAINROWS, 0 : 2 * W] = gain.astype(BF16)


def pair_kernel(
    x_ref, grad_ref, start_ref, b_ref, c_ref, col_ref, row_ref, enter_ref,
    inner_ref, grad_c_ref, grad_b_ref, sum_ref,
):
    b, c = b_ref[...], c_ref[...]
    scores = dot(b, c, 1, 1)
    causal = iota((T, T), 0) <= iota((T, T), 1)
    sum_ref[...] = jnp.zeros((T, T), F32)

    @pl.loop(0, H)
    def _(h):
        col = col_ref[h]
        differ = row_ref[pl.ds(h, 1), :] - jnp.concatenate([col, col], axis=1)
        table = jnp.exp(jnp.where(causal, differ, FAR))
        grad = grad_ref[:, lane(h)]
        inner_ref[:, lane(h)] = dot((scores * table).astype(BF16), grad)
        sum_ref[...] += dot(x_ref[:, lane(h)], grad, 1, 1) * table

    weights = sum_ref[...].astype(BF16)
    grad_b_ref[...] = dot(weights, c)

    def carried(h, total):
        return total + dot(start_ref[:, lane(h, 2 * W)], pair_state(enter_ref, h), 1, 1)

    grad_c_ref[...] = lax.fori_loop(0, H // 2, carried, dot(weights, b, 0, 0)).astype(BF16)


def last_kernel(
    inner_ref, leave_ref, b_ref, x_ref, end_ref, col_ref, grad_b_in, rate_ref, state_ref, enter_ref,
    grad_x_ref, grad_b_ref, decay_ref,
):
    b = b_ref[...]

    def step(h, carry):
        grad_b, rates, tail = carry
        cols = lane(h, 2 * W)
        leave = pair_state(leave_ref, h)
        col = pair_cols(col_ref, h)
        total = col[T - 1 : T, :]
        grad_x = inner_ref[:, cols] + jnp.exp(total - col) * dot(b, leave)
        grad_x_ref[:, cols] = grad_x.astype(BF16)
        rate = x_ref[:, cols].astype(F32) * grad_x
        at = iota((T, W), 1)
        rates = rates - jnp.where(at == 2 * h, row_sum(rate[:, :W]), 0.0)
        rates = rates - jnp.where(at == 2 * h + 1, row_sum(rate[:, W:]), 0.0)
        later = jnp.exp(total) * pair_state(enter_ref, h).astype(F32) + state_ref[:, cols]
        flow = jnp.sum(later * leave.astype(F32), axis=0, keepdims=True)
        at = iota((1, W), 1)
        tail = tail + jnp.where(at == 2 * h, row_sum(flow[:, :W]), 0.0)
        tail = tail + jnp.where(at == 2 * h + 1, row_sum(flow[:, W:]), 0.0)
        return grad_b + dot(end_ref[:, cols], leave, 1, 1), rates, tail

    start = (grad_b_in[...], rate_ref[...], jnp.zeros((1, W), F32))
    grad_b, rates, tail = lax.fori_loop(0, H // 2, step, start)
    grad_b_ref[...] = grad_b.astype(BF16)
    upper = (iota((T, T), 0) <= iota((T, T), 1)).astype(F32)
    decay_ref[...] = (dot(upper, rates, precision=HI) + tail)[:, :H]


def call(kernel, outs, args, scratch=(), smem=0, flops=0, cells=0):
    specs = [
        pl.BlockSpec(memory_space=pltpu.SMEM if i < smem else pltpu.VMEM) for i in range(len(args))
    ]
    moved = sum(a.size * a.dtype.itemsize for a in (*args, *outs))
    return pl.pallas_call(
        kernel,
        out_shape=outs,
        in_specs=specs,
        out_specs=[pl.BlockSpec(memory_space=pltpu.VMEM)] * len(outs),
        scratch_shapes=scratch,
        compiler_params=pltpu.CompilerParams(vmem_limit_bytes=48 * 2**20),
        cost_estimate=pl.CostEstimate(flops=flops, bytes_accessed=moved, transcendentals=cells),
    )(*args)


def shaped(shape, dtype=F32):
    return jax.ShapeDtypeStruct(shape, dtype)


def shift(value, axis, by):
    size = lax.axis_size(axis)
    return lax.ppermute(value, axis, [(i, (i + by) % size) for i in range(size)])


def gathered(value, axis):
    size, me = lax.axis_size(axis), lax.axis_index(axis)
    pieces = [shift(value, axis, k) if k else value for k in range(size - 1, -1, -1)]
    rows = value.shape[0]
    twice = jnp.concatenate(pieces + pieces, axis=0)
    return lax.dynamic_slice_in_dim(twice, lax.rem(2 * size - me - 1, size) * rows, size * rows, 0)


def exchange(value):
    return lax.all_to_all(value, SEQ_AXES, 0, 0, tiled=True)


def body(ssm, gate, state_in, state_out, log_decay, gain, out_weight, grad_rows):
    x, b, c = ssm[0], state_in[0], state_out[0]
    gate, grad_rows, gain_row = gate[0], grad_rows[0], gain[None]
    at = jnp.stack([lax.axis_index("x"), lax.axis_index("c")]).astype(jnp.int32)
    wide = shaped((T, INNER))
    wide_bf = shaped((T, INNER), BF16)
    states = shaped((SEQ, HALF, W), BF16)

    send, state, col, row, x_end = call(
        state_kernel,
        [shaped((SEQ, HALF + EXTRA, W), BF16), shaped((W, INNER)), shaped((H, T, W)), shaped((H, T)), wide_bf],
        [x, b, log_decay[0]],
        flops=2 * T * W * INNER,
        cells=T * INNER,
    )
    got = exchange(send)

    own = gathered(gathered(out_weight.T, "z"), "y")
    along = [own] + [shift(own, "x", k) for k in (1, 2, 3)]
    across = [shift(piece, "c", 1) for piece in along]

    [inner] = call(
        inner_kernel, [wide], [x, b, c, col, row], flops=2 * T * T * INNER, cells=T * T * H
    )
    enter_part, factor = call(forward_scan_kernel, [states, shaped((SEQ, W))], [got])
    enter = exchange(enter_part)
    [grad_normed] = call(
        normed_grad_kernel, [wide], [at, grad_rows, *along, *across], smem=1, flops=2 * T * D * INNER
    )
    grad_gate, grad_y, grad_start, normed, grad_send, gain_term, rate = call(
        norm_kernel,
        [wide_bf, wide_bf, wide_bf, wide_bf, states, shaped((1, INNER)), shaped((T, W))],
        [inner, grad_normed, gate, enter, c, col, gain_row],
        scratch=[pltpu.VMEM((T, INNER), F32), pltpu.VMEM((T, INNER), F32)],
        flops=4 * T * W * INNER,
        cells=4 * T * INNER,
    )
    grad_got = exchange(grad_send)
    terms = call(
        weight_kernel,
        [shaped((W + GAINROWS, INNER), BF16)] * 8,
        [at, grad_rows, normed, gain_term],
        smem=1,
        flops=2 * T * D * INNER,
    )
    halves = [
        terms[k].astype(F32) + shift(terms[4 + k], "c", 1).astype(F32) for k in range(4)
    ]
    quarter = halves[0] + sum(
        shift(halves[k].astype(BF16), "x", k).astype(F32) for k in (1, 2, 3)
    )
    grad_inner, grad_state_out, grad_b = call(
        pair_kernel,
        [wide, shaped((T, W), BF16), shaped((T, W))],
        [x, grad_y, grad_start, b, c, col, row, enter],
        scratch=[pltpu.VMEM((T, T), F32)],
        flops=5 * T * T * INNER,
        cells=T * T * H,
    )
    [leave_part] = call(backward_scan_kernel, [states], [grad_got, factor])
    leave = exchange(leave_part)
    rows = quarter[:W].astype(BF16).reshape(SEQ, HALF, W)
    gains = jnp.pad(quarter[W, : 2 * W].astype(BF16).reshape(SEQ, 1, 8), ((0, 0), (0, 7), (0, W - 8)))
    final = jnp.sum(exchange(jnp.concatenate([rows, gains], axis=1)).astype(F32), axis=0)
    grad_input, grad_state_in, grad_log_decay = call(
        last_kernel,
        [wide_bf, shaped((T, W), BF16), shaped((T, H))],
        [grad_inner, leave, b, x, x_end, col, grad_b, rate, state, enter],
        flops=4 * T * W * INNER,
        cells=T * INNER,
    )
    return (
        grad_input[None],
        grad_gate[None],
        grad_state_in[None],
        grad_state_out[None],
        grad_log_decay[None],
        final[:HALF].reshape(4, INNER),
        final[HALF, :8],
    )


def solution(mesh):
    split = Mesh(mesh.devices.reshape(4, 2, 4, 8), ("x", "c", "y", "z"))
    shower, seq = ("x", "c"), ("y", "z")
    rows = P(shower, seq, None)
    every = (*shower, *seq)
    return jax.shard_map(
        body,
        mesh=split,
        in_specs=(rows, rows, rows, rows, rows, P(), P(None, every), rows),
        out_specs=(rows, rows, rows, rows, rows, P(every, None), P(every)),
        check_vma=False,
    )
```

```python
import math

import jax
import jax.numpy as jnp
from jax import lax
from jax.experimental import pallas as pl
from jax.experimental.pallas import tpu as pltpu
from jax.sharding import Mesh
from jax.sharding import PartitionSpec as P

F32, BF16 = jnp.float32, jnp.bfloat16
T = 256
H = 16
W = 128
INNER = H * W
D = 1024
SEQ = 32
HALF = 64
EXTRA = 16
GAINROWS = 16
SEQ_AXES = ("y", "z")
FAR = -1e30
HI = lax.Precision.HIGHEST


def lane(h, width=W):
    return pl.ds(pl.multiple_of(h * width, width), width)


def dot(a, b, ca=1, cb=0, precision=None):
    return lax.dot_general(
        a, b, (((ca,), (cb,)), ((), ())), precision=precision, preferred_element_type=F32
    )


def iota(shape, axis):
    return lax.broadcasted_iota(jnp.int32, shape, axis)


def row_sum(a):
    return jnp.sum(a, axis=1, keepdims=True)


def column(ref, h):
    return jnp.broadcast_to(ref[pl.ds(h, 1), :], (W, T)).T


def pair_cols(ref, h):
    return jnp.concatenate([column(ref, 2 * h), column(ref, 2 * h + 1)], axis=1)


def pair_state(ref, h):
    blocks = ref[pl.ds(4 * h, 4), 0:HALF, :]
    first = blocks[0:2].reshape(W, W)
    second = blocks[2:4].reshape(W, W)
    return jnp.concatenate([first, second], axis=1)


def split_state(ref, h, value):
    ref[pl.ds(4 * h, 2), 0:HALF, :] = value[:, :W].reshape(2, HALF, W)
    ref[pl.ds(4 * h + 2, 2), 0:HALF, :] = value[:, W:].reshape(2, HALF, W)


def state_kernel(flow, x_ref, b_ref, decay_ref, send_ref, row_ref):
    tri = (iota((T, T), 0) >= iota((T, T), 1)).astype(F32)
    flow.arrive()
    decay = decay_ref[...]
    row_ref[...] = dot(decay, tri, 1, 1, precision=HI)
    flow.leave()
    b = b_ref[...]

    @pl.loop(0, H // 2)
    def _(h):
        flow.arrive(h)
        col = pair_cols(row_ref, h)
        total = col[T - 1 : T, :]
        cols = lane(h, 2 * W)
        x_end = (x_ref[:, cols].astype(F32) * jnp.exp(total - col)).astype(BF16)
        split_state(send_ref, h, dot(b, x_end, 0, 0).astype(BF16))
        high = total.astype(BF16).astype(F32)
        middle = (total - high).astype(BF16).astype(F32)
        low = total - high - middle
        at = iota((EXTRA, 2 * W), 0)
        rows = jnp.where(at == 0, high, jnp.where(at == 1, middle, jnp.where(at == 2, low, 0.0)))
        rows = rows.astype(BF16)
        for k in range(4):
            half = rows[:, :W] if k < 2 else rows[:, W:]
            send_ref[4 * h + k, HALF : HALF + EXTRA, :] = half
        flow.leave(h)


def forward_scan_kernel(flow, got_ref, out_ref, factor_ref):
    group = SEQ // PAIRS

    def step(h, carry):
        flow.arrive(h)
        for k in range(group):
            j = h * group + k
            out_ref[j] = carry.astype(BF16)
            tail = got_ref[j, HALF : HALF + EXTRA, :].astype(F32)
            factor = jnp.exp(jnp.sum(tail, axis=0, keepdims=True))
            factor_ref[pl.ds(j, 1), :] = factor
            carry = factor * carry + got_ref[j, 0:HALF, :].astype(F32)
        flow.leave(h)
        return carry

    lax.fori_loop(0, PAIRS, step, jnp.zeros((HALF, W), F32))
    flow.leave()


def backward_scan_kernel(flow, got_ref, factor_ref, out_ref):
    group = SEQ // PAIRS
    flow.arrive()

    def step(i, carry):
        h = PAIRS - 1 - i
        flow.arrive(h, True)
        for k in range(group - 1, -1, -1):
            j = h * group + k
            out_ref[j] = carry.astype(BF16)
            carry = factor_ref[pl.ds(j, 1), :] * carry + got_ref[j].astype(F32)
        flow.leave(h, True)
        return carry

    lax.fori_loop(0, PAIRS, step, jnp.zeros((HALF, W), F32))


def inner_kernel(flow, x_ref, b_ref, c_ref, row_ref, inner_ref):
    flow.arrive()
    scores = dot(c_ref[...], b_ref[...], 1, 1)
    causal = iota((T, T), 0) >= iota((T, T), 1)

    @pl.loop(0, PAIRS)
    def _(pair):
        flow.arrive(pair)
        for h in (2 * pair, 2 * pair + 1):
            col = column(row_ref, h)
            differ = jnp.concatenate([col, col], axis=1) - row_ref[pl.ds(h, 1), :]
            kernel = (scores * jnp.exp(jnp.where(causal, differ, FAR))).astype(BF16)
            inner_ref[:, lane(h)] = dot(kernel, x_ref[:, lane(h)])
        flow.leave(pair)


def order_kernel(flow, at_ref, *refs):
    pieces, (_, sems) = refs[:4], refs[4:]
    target = flow.outgoing.pairs.pop()[1]
    copies = []
    for k, piece in enumerate(pieces):
        rows = pl.multiple_of(lax.rem(at_ref[2] + 4 - k, 4) * HALF, HALF)
        copies.append(pltpu.make_async_copy(piece, target.at[pl.ds(rows, HALF), :], sems.at[k, 0]))
        copies[k].start()
    for copy in copies:
        copy.wait()


def normed_grad_kernel(flow, at_ref, grad_far, *refs):
    pieces, (out_ref, grad_ref, weight_ref, sems) = refs[:8], refs[8:]
    x, c = at_ref[0], at_ref[1]
    copies = [pltpu.make_async_copy(grad_far, grad_ref, sems.at[0, 0])]
    for k, piece in enumerate(pieces):
        copies.append(pltpu.make_async_copy(piece, weight_ref.at[k], sems.at[1 + k, 0]))
    for copy in copies:
        copy.start()
    copies[0].wait()
    for core in range(2):
        for k in range(4):
            copies[1 + 4 * core + k].wait()
            block = lax.rem(x + 4 - k, 4) * 2 + (c if core == 0 else 1 - c)
            out_ref[:, lane(block, 2 * W)] = dot(grad_ref[...], weight_ref[4 * core + k], 1, 1).astype(BF16)
    for h in range(CHUNKS):
        for k in flow.outgoing.where(True):
            flow.outgoing.copy(k, h).start()


def norm_kernel(
    flow, inner_ref, gn_ref, gate_ref, enter_ref, c_ref, row_ref, gain_ref,
    gate_out, grad_out, start_out, normed_out, send_ref, gain_out, rate_out, y_ref, u_ref,
):
    flow.arrive()
    c = c_ref[...]

    def first(h, sums):
        flow.arrive(h)
        squares, mixed = sums
        cols = lane(h, 2 * W)
        keep = jnp.exp(pair_cols(row_ref, h))
        y = inner_ref[:, cols] + keep * dot(c, pair_state(enter_ref, h))
        gate = gate_ref[:, cols].astype(F32)
        u = y * (gate * jax.nn.sigmoid(gate))
        y_ref[:, cols] = y
        u_ref[:, cols] = u
        both = gain_ref[:, cols] * gn_ref[:, cols].astype(F32) * u
        squared = u * u
        return (
            squares + squared[:, :W] + squared[:, W:],
            mixed + both[:, :W] + both[:, W:],
        )

    zero = jnp.zeros((T, W), F32)
    squares, mixed = lax.fori_loop(0, H // 2, first, (zero, zero))
    rstd = lax.rsqrt(row_sum(squares) / INNER + 1e-5)
    pull = rstd * rstd * rstd * (row_sum(mixed) / INNER)
    rate_out[...] = zero

    @pl.loop(0, H // 2)
    def _(h):
        cols = lane(h, 2 * W)
        y, u, gn = y_ref[:, cols], u_ref[:, cols], gn_ref[:, cols].astype(F32)
        gain = gain_ref[:, cols]
        gate = gate_ref[:, cols].astype(F32)
        sig = jax.nn.sigmoid(gate)
        normal = u * rstd
        grad_u = rstd * (gain * gn) - u * pull
        grad_y = grad_u * (gate * sig)
        gate_out[:, cols] = (grad_u * y * sig * (1.0 + gate * (1.0 - sig))).astype(BF16)
        normed_out[:, cols] = (normal * gain).astype(BF16)
        gain_out[:, cols] = jnp.sum(gn * normal, axis=0, keepdims=True)
        grad_out[:, cols] = grad_y.astype(BF16)
        start = (grad_y * jnp.exp(pair_cols(row_ref, h))).astype(BF16)
        start_out[:, cols] = start
        rate = grad_y * y
        at = iota((T, W), 1)
        rates = rate_out[...]
        rates = jnp.where(at == 2 * h, row_sum(rate[:, :W]), rates)
        rate_out[...] = jnp.where(at == 2 * h + 1, row_sum(rate[:, W:]), rates)
        split_state(send_ref, h, dot(c, start, 0, 0).astype(BF16))
        flow.leave(h)

    flow.leave()


def weight_kernel(flow, at_ref, grad_ref, normed_ref, gain_ref, own_ref, other_ref):
    x, c = at_ref[0], at_ref[1]
    flow.arrive()
    for h in range(0, PAIRS, STEP):
        flow.arrive(h)
    normed = normed_ref[...]
    for at, out, core in ((1, other_ref, 1 - c), (0, own_ref, c)):
        for k in range(4):
            block = lax.rem(x + k, 4) * 2 + core
            out[k, 0:W, :] = dot(grad_ref[:, lane(block)], normed, 0, 0).astype(BF16)
            gain = jnp.broadcast_to(gain_ref[:, lane(block, 2 * W)], (GAINROWS, 2 * W))
            out[k, W : W + GAINROWS, :] = jnp.zeros((GAINROWS, INNER), BF16)
            out[k, W : W + GAINROWS, 0 : 2 * W] = gain.astype(BF16)
            flow.outgoing.copy(at, k).start()


def add_kernel(flow, own_term, other_term, own_ref, right_ref, left_ref, forth_ref, back_ref):
    for at, k in ((3, 2), (1, 1), (2, 3), (0, 0)):
        flow.arrive(k * STEP)
        total = (own_term[k].astype(F32) + other_term[k].astype(F32)).astype(BF16)
        if k == 2:
            forth_ref[...] = total[:, :D]
            back_ref[...] = total[:, D:]
            flow.outgoing.copy(4).start()
        else:
            (own_ref, right_ref, left_ref)[at][...] = total
        flow.outgoing.copy(at).start()


def relay_kernel(flow, right_in, left_in, forth_in, back_in, right_ref, left_ref):
    flow.arrive()
    right_ref[:, :D] = (right_in[:, :D].astype(F32) + forth_in[...].astype(F32)).astype(BF16)
    right_ref[:, D:] = right_in[:, D:]
    left_ref[:, :D] = left_in[:, :D]
    left_ref[:, D:] = (left_in[:, D:].astype(F32) + back_in[...].astype(F32)).astype(BF16)
    flow.leave()


def pair_kernel(
    flow, x_ref, grad_ref, start_ref, b_ref, c_ref, row_ref, enter_ref,
    inner_ref, grad_c_ref, grad_b_ref, sum_ref,
):
    flow.arrive()
    b, c = b_ref[...], c_ref[...]
    scores = dot(b, c, 1, 1)
    causal = iota((T, T), 0) <= iota((T, T), 1)
    sum_ref[...] = jnp.zeros((T, T), F32)

    def step(pair, total):
        flow.arrive(pair)
        weights = []
        for h in (2 * pair, 2 * pair + 1):
            col = column(row_ref, h)
            differ = row_ref[pl.ds(h, 1), :] - jnp.concatenate([col, col], axis=1)
            table = jnp.exp(jnp.where(causal, differ, FAR))
            grad = grad_ref[:, lane(h)]
            inner_ref[:, lane(h)] = dot((scores * table).astype(BF16), grad)
            weights.append(dot(x_ref[:, lane(h)], grad, 1, 1) * table)
        sum_ref[...] += weights[0] + weights[1]
        flow.leave(pair)
        return total + dot(start_ref[:, lane(pair, 2 * W)], pair_state(enter_ref, pair), 1, 1)

    carried = lax.fori_loop(0, PAIRS, step, jnp.zeros((T, W), F32))
    weights = sum_ref[...].astype(BF16)
    grad_b_ref[...] = dot(weights, c)
    grad_c_ref[...] = (carried + dot(weights, b, 0, 0)).astype(BF16)
    flow.leave()


def sum_kernel(flow, *refs):
    *terms, out_ref, gain_ref = refs
    flow.arrive()
    total = terms[0][...].astype(F32)
    for term in terms[1:]:
        total = total + term[...].astype(F32)
    out_ref[...] = total[0:W, :].astype(BF16)
    gain_ref[...] = total[W : W + 8, 0 : 2 * W]
    flow.leave()


def last_kernel(
    flow, inner_ref, leave_ref, b_ref, x_ref, row_ref, grad_b_in, rate_ref, state_ref, enter_ref,
    grad_x_ref, grad_b_ref, decay_ref,
):
    flow.arrive()
    b = b_ref[...]

    def step(h, carry):
        flow.arrive(h)
        grad_b, rates, tail = carry
        cols = lane(h, 2 * W)
        leave = pair_state(leave_ref, h)
        col = pair_cols(row_ref, h)
        total = col[T - 1 : T, :]
        keep = jnp.exp(total - col)
        grad_x = inner_ref[:, cols] + keep * dot(b, leave)
        grad_x_ref[:, cols] = grad_x.astype(BF16)
        flow.leave(h)
        x = x_ref[:, cols].astype(F32)
        rate = x * grad_x
        at = iota((T, W), 1)
        rates = rates - jnp.where(at == 2 * h, row_sum(rate[:, :W]), 0.0)
        rates = rates - jnp.where(at == 2 * h + 1, row_sum(rate[:, W:]), 0.0)
        state = pair_state(state_ref, h).astype(F32)
        later = jnp.exp(total) * pair_state(enter_ref, h).astype(F32) + state
        across = jnp.sum(later * leave.astype(F32), axis=0, keepdims=True)
        at = iota((W, 1), 0)
        tail = tail + jnp.where(at == 2 * h, row_sum(across[:, :W]), 0.0)
        tail = tail + jnp.where(at == 2 * h + 1, row_sum(across[:, W:]), 0.0)
        return grad_b + dot((x * keep).astype(BF16), leave, 1, 1), rates, tail

    start = (grad_b_in[...], rate_ref[...], jnp.zeros((W, 1), F32))
    grad_b, rates, tail = lax.fori_loop(0, H // 2, step, start)
    grad_b_ref[...] = grad_b.astype(BF16)
    lower = (iota((T, T), 0) >= iota((T, T), 1)).astype(F32)
    decay_ref[...] = (dot(rates, lower, 0, 0, precision=HI) + tail)[:H, :]
    flow.leave()


PAIRS = H // 2
CHUNKS = 4
STEP = PAIRS // CHUNKS


def chunked(array):
    return array.shape == (T, INNER) or len(array.shape) == 3 and array.shape[0] in (4, SEQ)


def part(ref, h):
    if len(ref.shape) == 2:
        return ref.at[:, lane(h, 2 * W * STEP)]
    count = ref.shape[0] // CHUNKS
    return ref.at[pl.ds(h * count, count)]


class Traffic:
    def __init__(self, sources, targets, sems):
        self.pairs = list(zip(sources, targets, range(len(sources))))
        self.sems = sems

    def copy(self, k, h=None):
        source, target, at = self.pairs[k]
        if h is None:
            return pltpu.make_async_copy(source, target, self.sems.at[at, 0])
        return pltpu.make_async_copy(part(source, h), part(target, h), self.sems.at[at, h])

    def where(self, pieces):
        return [k for k, (source, _, _) in enumerate(self.pairs) if chunked(source) == pieces]


class Flow:
    def __init__(self, incoming, outgoing):
        self.incoming, self.outgoing = incoming, outgoing

    def begin(self):
        for k in self.incoming.where(False):
            self.incoming.copy(k).start()
        for h in range(CHUNKS):
            for k in self.incoming.where(True):
                self.incoming.copy(k, h).start()

    def arrive(self, pair=None, last_first=False):
        if pair is None:
            for k in self.incoming.where(False):
                self.incoming.copy(k).wait()
            return

        @pl.when(lax.rem(pair, STEP) == (STEP - 1 if last_first else 0))
        def _():
            for k in self.incoming.where(True):
                self.incoming.copy(k, lax.div(pair, STEP)).wait()

    def leave(self, pair=None, last_first=False):
        if pair is None:
            for k in self.outgoing.where(False):
                self.outgoing.copy(k).start()
            return

        @pl.when(lax.rem(pair, STEP) == (0 if last_first else STEP - 1))
        def _():
            for k in self.outgoing.where(True):
                self.outgoing.copy(k, lax.div(pair, STEP)).start()

    def end(self):
        for k in self.outgoing.where(False):
            self.outgoing.copy(k).wait()
        for h in range(CHUNKS):
            for k in self.outgoing.where(True):
                self.outgoing.copy(k, h).wait()


def call(kernel, outs, args, scratch=(), smem=0, us=1.0, loose=(), after=(), own=False):
    scalars, arrays = args[:smem], args[smem:]
    far = pl.BlockSpec(memory_space=pltpu.HBM)
    moved = sum(a.size * a.dtype.itemsize for a in (*args, *outs))
    held = moved + sum(math.prod(s.shape) * 4 for s in scratch)
    kept = [] if own else arrays
    counts = (smem, len(arrays), len(after), len(outs), len(kept), len(outs), len(scratch))

    def run(*refs):
        groups = []
        for count in counts:
            groups.append(refs[:count])
            refs = refs[count:]
        numbers, sources, _, targets, near_in, near_out, rest = groups
        flow = Flow(Traffic(sources, near_in, refs[0]), Traffic(near_out, targets, refs[1]))
        if own:
            kernel(flow, *numbers, *sources, *near_out, *rest, refs[0])
        else:
            flow.begin()
            kernel(flow, *numbers, *near_in, *near_out, *rest)
        flow.end()

    tied = [a if any(a is b for b in loose) else pltpu.with_memory_space_constraint(a, pltpu.HBM) for a in arrays]
    return pl.pallas_call(
        run,
        out_shape=[pltpu.HBM(out.shape, out.dtype) for out in outs],
        in_specs=[pl.BlockSpec(memory_space=pltpu.SMEM)] * smem
        + [pl.BlockSpec(memory_space=pl.ANY) if any(a is b for b in loose) else far for a in arrays]
        + [pl.BlockSpec(memory_space=pl.ANY)] * len(after),
        out_specs=[far] * len(outs),
        scratch_shapes=[
            *(pltpu.VMEM(a.shape, a.dtype) for a in (*kept, *outs)),
            *scratch,
            pltpu.SemaphoreType.DMA((len(arrays), CHUNKS)),
            pltpu.SemaphoreType.DMA((len(outs), CHUNKS)),
        ],
        compiler_params=pltpu.CompilerParams(vmem_limit_bytes=held + 6 * 2**20),
        cost_estimate=pl.CostEstimate(flops=int(us * 1.1e9), bytes_accessed=moved, transcendentals=0),
    )(*scalars, *tied, *after)


def shaped(shape, dtype=F32):
    return jax.ShapeDtypeStruct(shape, dtype)


def shift(value, axis, by):
    size = lax.axis_size(axis)
    return lax.ppermute(value, axis, [(i, (i + by) % size) for i in range(size)])


def shifts(values, axis):
    return [value if k == 0 else shift(value, axis, k) for k, value in enumerate(values)]


def exchange(value, axes=SEQ_AXES):
    return lax.all_to_all(value, axes, 0, 0, tiled=True)


def body(ssm, gate, state_in, state_out, log_decay, gain, out_weight, grad_rows):
    x, b, c = ssm[0], state_in[0], state_out[0]
    gate, grad_rows, gain_row = gate[0], grad_rows[0], gain[None]
    at = jnp.stack([lax.axis_index(name) for name in ("x", "c", "y")]).astype(jnp.int32)
    wide = shaped((T, INNER))
    wide_bf = shaped((T, INNER), BF16)
    states = shaped((SEQ, HALF, W), BF16)

    send, row = call(
        state_kernel,
        [shaped((SEQ, HALF + EXTRA, W), BF16), shaped((H, T))],
        [x, b, log_decay[0].T],
        us=0.1,
    )
    got = exchange(send)

    own = exchange(jnp.broadcast_to(out_weight.T, (8, 8, D)), "z").reshape(HALF, D)
    [inner] = call(inner_kernel, [wide], [x, b, c, row], us=0.3)
    slices = shifts([own] * 4, "y")
    [ordered] = call(
        order_kernel, [shaped((T, D), BF16)], [at, *slices], smem=1, us=0.1, loose=slices, own=True, after=[inner]
    )
    pieces = shifts([ordered] * 4, "x")
    pieces += [shift(piece, "c", 1) for piece in pieces]

    enter_part, factor = call(
        forward_scan_kernel, [states, shaped((SEQ, W))], [got], us=0.1, loose=[got]
    )
    enter = exchange(enter_part)
    [grad_normed] = call(
        normed_grad_kernel,
        [wide_bf],
        [at, grad_rows, *pieces],
        scratch=[pltpu.VMEM((T, D), BF16), pltpu.VMEM((8, T, D), BF16)],
        own=True,
        smem=1,
        us=1.0,
        loose=pieces,
    )
    grad_gate, grad_y, grad_start, normed, grad_send, gain_term, rate = call(
        norm_kernel,
        [wide_bf, wide_bf, wide_bf, wide_bf, states, shaped((1, INNER)), shaped((T, W))],
        [inner, grad_normed, gate, enter, c, row, gain_row],
        scratch=[pltpu.VMEM((T, INNER), F32), pltpu.VMEM((T, INNER), F32)],
        us=0.3,
        loose=[enter],
    )
    grad_got = exchange(grad_send)
    own_term, other_term = call(
        weight_kernel,
        [shaped((4, W + GAINROWS, INNER), BF16)] * 2,
        [at, grad_rows, normed, gain_term],
        smem=1,
        us=4.6,
    )
    other_term = shift(other_term, "c", 1)
    block = shaped((W + GAINROWS, INNER), BF16)
    half = shaped((W + GAINROWS, D), BF16)
    kept, right, left, forth, back = call(
        add_kernel, [block, block, block, half, half], [own_term, other_term], us=3.7, loose=[other_term]
    )
    forth, back = shift(forth, "x", 1), shift(back, "x", -1)
    right, left = call(
        relay_kernel, [block, block], [right, left, forth, back], us=2.8, loose=[forth, back]
    )
    [leave_part] = call(
        backward_scan_kernel, [states], [grad_got, factor], us=2.0, loose=[grad_got], after=[right]
    )
    leave = exchange(leave_part)
    right, left = shift(right, "x", 1), shift(left, "x", -1)
    quarter, gains = call(
        sum_kernel,
        [shaped((W, INNER), BF16), shaped((8, 2 * W))],
        [kept, right, left],
        us=2.6,
        loose=[right, left],
    )
    grad_inner, grad_state_out, grad_b = call(
        pair_kernel,
        [wide, shaped((T, W), BF16), shaped((T, W))],
        [x, grad_y, grad_start, b, c, row, enter],
        scratch=[pltpu.VMEM((T, T), F32)],
        us=5.8,
        loose=[enter],
        after=[leave_part],
    )
    rows = quarter.reshape(SEQ, HALF, W)
    gains = jnp.pad(gains[0].astype(BF16).reshape(SEQ, 1, 8), ((0, 0), (0, 7), (0, W - 8)))
    final = jnp.sum(exchange(jnp.concatenate([rows, gains], axis=1)).astype(F32), axis=0)
    grad_input, grad_state_in, grad_log_decay = call(
        last_kernel,
        [wide_bf, shaped((T, W), BF16), shaped((H, T))],
        [grad_inner, leave, b, x, row, grad_b, rate, send, enter],
        us=5.5,
        loose=[leave, enter],
    )
    return (
        grad_input[None],
        grad_gate[None],
        grad_state_in[None],
        grad_state_out[None],
        grad_log_decay.T[None],
        final[:HALF].reshape(4, INNER),
        final[HALF, :8],
    )


def solution(mesh):
    split = Mesh(mesh.devices.reshape(4, 2, 4, 8), ("x", "c", "y", "z"))
    shower, seq = ("x", "c"), ("y", "z")
    rows = P(shower, seq, None)
    every = (*shower, *seq)
    return jax.shard_map(
        body,
        mesh=split,
        in_specs=(rows, rows, rows, rows, rows, P(), P(None, every), rows),
        out_specs=(rows, rows, rows, rows, rows, P(every, None), P(every)),
        check_vma=False,
    )
```

```python
import math

import jax
import jax.numpy as jnp
from jax import lax
from jax.experimental import pallas as pl
from jax.experimental.pallas import tpu as pltpu
from jax.sharding import Mesh
from jax.sharding import PartitionSpec as P

F32, BF16 = jnp.float32, jnp.bfloat16
T = 256
H = 16
W = 128
INNER = H * W
D = 1024
SEQ = 32
HALF = 64
EXTRA = 16
GAINROWS = 16
SEQ_AXES = ("y", "z")
FAR = -1e30
FAR_PIECES = (0, 4, 1, 3)
HI = lax.Precision.HIGHEST


def lane(h, width=W):
    return pl.ds(pl.multiple_of(h * width, width), width)


def dot(a, b, ca=1, cb=0, precision=None):
    return lax.dot_general(
        a, b, (((ca,), (cb,)), ((), ())), precision=precision, preferred_element_type=F32
    )


def iota(shape, axis):
    return lax.broadcasted_iota(jnp.int32, shape, axis)


def row_sum(a):
    return jnp.sum(a, axis=1, keepdims=True)


def column(row):
    return jnp.broadcast_to(row, (W, T)).T


def row_of(ref, h):
    return ref[pl.ds(h, 1), :]


def pair_starts(ref, h):
    return jnp.concatenate([column(jnp.exp(row_of(ref, 2 * h + k))) for k in range(2)], axis=1)


def pair_ends(ref, h):
    rows = [row_of(ref, 2 * h + k) for k in range(2)]
    keep = jnp.concatenate([column(jnp.exp(row[:, T - 1 :] - row)) for row in rows], axis=1)
    total = jnp.concatenate([jnp.broadcast_to(row[:, T - 1 :], (1, W)) for row in rows], axis=1)
    return keep, total


def pair_state(ref, h):
    blocks = ref[pl.ds(4 * h, 4), 0:HALF, :]
    first = blocks[0:2].reshape(W, W)
    second = blocks[2:4].reshape(W, W)
    return jnp.concatenate([first, second], axis=1)


def split_state(ref, h, value):
    ref[pl.ds(4 * h, 2), 0:HALF, :] = value[:, :W].reshape(2, HALF, W)
    ref[pl.ds(4 * h + 2, 2), 0:HALF, :] = value[:, W:].reshape(2, HALF, W)


def state_kernel(flow, x_ref, b_ref, decay_ref, send_ref, row_ref):
    tri = (iota((T, T), 0) >= iota((T, T), 1)).astype(F32)
    flow.arrive()
    decay = decay_ref[...]
    row_ref[...] = dot(decay, tri, 1, 1, precision=HI)
    flow.leave()
    b = b_ref[...]

    @pl.loop(0, H // 2)
    def _(h):
        flow.arrive(h)
        keep, total = pair_ends(row_ref, h)
        cols = lane(h, 2 * W)
        x_end = (x_ref[:, cols].astype(F32) * keep).astype(BF16)
        split_state(send_ref, h, dot(b, x_end, 0, 0).astype(BF16))
        high = total.astype(BF16).astype(F32)
        middle = (total - high).astype(BF16).astype(F32)
        low = total - high - middle
        at = iota((EXTRA, 2 * W), 0)
        rows = jnp.where(at == 0, high, jnp.where(at == 1, middle, jnp.where(at == 2, low, 0.0)))
        rows = rows.astype(BF16)
        for k in range(4):
            half = rows[:, :W] if k < 2 else rows[:, W:]
            send_ref[4 * h + k, HALF : HALF + EXTRA, :] = half
        flow.leave(h)


def forward_scan_kernel(flow, got_ref, out_ref, factor_ref):
    group = SEQ // PAIRS

    def step(h, carry):
        flow.arrive(h)
        for k in range(group):
            j = h * group + k
            out_ref[j] = carry.astype(BF16)
            tail = got_ref[j, HALF : HALF + EXTRA, :].astype(F32)
            factor = jnp.exp(jnp.sum(tail, axis=0, keepdims=True))
            factor_ref[pl.ds(j, 1), :] = factor
            carry = factor * carry + got_ref[j, 0:HALF, :].astype(F32)
        flow.leave(h)
        return carry

    lax.fori_loop(0, PAIRS, step, jnp.zeros((HALF, W), F32))
    flow.leave()


def backward_scan_kernel(flow, got_ref, factor_ref, out_ref):
    group = SEQ // PAIRS
    flow.arrive()

    def step(i, carry):
        h = PAIRS - 1 - i
        flow.arrive(h, True)
        for k in range(group - 1, -1, -1):
            j = h * group + k
            out_ref[j] = carry.astype(BF16)
            carry = factor_ref[pl.ds(j, 1), :] * carry + got_ref[j].astype(F32)
        flow.leave(h, True)
        return carry

    lax.fori_loop(0, PAIRS, step, jnp.zeros((HALF, W), F32))


def inner_kernel(flow, x_ref, b_ref, c_ref, row_ref, inner_ref):
    flow.arrive()
    scores = dot(c_ref[...], b_ref[...], 1, 1)
    causal = iota((T, T), 0) >= iota((T, T), 1)

    @pl.loop(0, PAIRS)
    def _(pair):
        flow.arrive(pair)
        for h in (2 * pair, 2 * pair + 1):
            col = column(row_of(row_ref, h))
            differ = jnp.concatenate([col, col], axis=1) - row_of(row_ref, h)
            kernel = (scores * jnp.exp(jnp.where(causal, differ, FAR))).astype(BF16)
            inner_ref[:, lane(h)] = dot(kernel, x_ref[:, lane(h)]).astype(BF16)
        flow.leave(pair)


def order_kernel(flow, at_ref, *refs):
    pieces, (_, sems) = refs[:4], refs[4:]
    target = flow.outgoing.pairs.pop()[1]
    copies = []
    for k, piece in enumerate(pieces):
        rows = pl.multiple_of(lax.rem(at_ref[2] + 4 - k, 4) * HALF, HALF)
        copies.append(pltpu.make_async_copy(piece, target.at[pl.ds(rows, HALF), :], sems.at[k, 0]))
        copies[k].start()
    for copy in copies:
        copy.wait()


def normed_grad_kernel(flow, at_ref, grad_far, *refs):
    pieces, (out_ref, grad_ref, weight_ref, sems) = refs[:8], refs[8:]
    x, c = at_ref[0], at_ref[1]
    grad_copy = pltpu.make_async_copy(grad_far, grad_ref, sems.at[0, 0])
    grad_copy.start()
    copies = {}
    for slot, at in enumerate(FAR_PIECES):
        copies[at] = (pltpu.make_async_copy(pieces[at], weight_ref.at[slot], sems.at[1 + slot, 0]), slot)
        copies[at][0].start()
    grad_copy.wait()
    for at in (*(k for k in range(8) if k not in FAR_PIECES), *FAR_PIECES):
        if at in copies:
            copies[at][0].wait()
        weight = weight_ref[copies[at][1]] if at in copies else pieces[at][...]
        block = lax.rem(x + 4 - at % 4, 4) * 2 + (c if at < 4 else 1 - c)
        out_ref[:, lane(block, 2 * W)] = dot(grad_ref[...], weight, 1, 1).astype(BF16)
    for h in range(CHUNKS):
        for k in flow.outgoing.where(True):
            flow.outgoing.copy(k, h).start()


def norm_kernel(
    flow, at_ref, inner_ref, gn_ref, gate_ref, enter_ref, c_ref, row_ref, gain_ref, rows_ref,
    gate_out, grad_out, send_ref, rate_out, own_ref, other_ref, y_ref, sig_ref, normed_out, gain_out,
):
    flow.arrive()
    c = c_ref[...]

    def first(h, sums):
        flow.arrive(h)
        squares, mixed = sums
        cols = lane(h, 2 * W)
        keep = pair_starts(row_ref, h)
        y = inner_ref[:, cols].astype(F32) + keep * dot(c, pair_state(enter_ref, h))
        gate = gate_ref[:, cols].astype(F32)
        sig = 0.5 * jnp.tanh(0.5 * gate) + 0.5
        u = y * (gate * sig)
        y_ref[:, cols] = y
        sig_ref[:, cols] = sig
        both = gain_ref[:, cols] * gn_ref[:, cols].astype(F32) * u
        squared = u * u
        return (
            squares + squared[:, :W] + squared[:, W:],
            mixed + both[:, :W] + both[:, W:],
        )

    zero = jnp.zeros((T, W), F32)
    squares, mixed = lax.fori_loop(0, H // 2, first, (zero, zero))
    rstd = lax.rsqrt(row_sum(squares) / INNER + 1e-5)
    pull = rstd * rstd * rstd * (row_sum(mixed) / INNER)
    rate_out[...] = zero

    @pl.loop(0, H // 2)
    def _(h):
        cols = lane(h, 2 * W)
        y, sig, gn = y_ref[:, cols], sig_ref[:, cols], gn_ref[:, cols].astype(F32)
        gain = gain_ref[:, cols]
        gate = gate_ref[:, cols].astype(F32)
        active = gate * sig
        u = y * active
        normal = u * rstd
        grad_u = rstd * (gain * gn) - u * pull
        grad_y = grad_u * active
        gate_out[:, cols] = (grad_u * y * (sig + active * (1.0 - sig))).astype(BF16)
        normed_out[:, cols] = (normal * gain).astype(BF16)
        gain_out[:, cols] = jnp.sum(gn * normal, axis=0, keepdims=True)
        grad_out[:, cols] = grad_y.astype(BF16)
        start = (grad_y * pair_starts(row_ref, h)).astype(BF16)
        rate = grad_y * y
        at = iota((T, W), 1)
        rates = rate_out[...]
        rates = jnp.where(at == 2 * h, row_sum(rate[:, :W]), rates)
        rate_out[...] = jnp.where(at == 2 * h + 1, row_sum(rate[:, W:]), rates)
        split_state(send_ref, h, dot(c, start, 0, 0).astype(BF16))
        flow.leave(h)

    flow.leave()
    x, core = at_ref[0], at_ref[1]
    normed = normed_out[...]
    for at, out, target in ((5, other_ref, 1 - core), (4, own_ref, core)):
        for k in range(4):
            block = lax.rem(x + k, 4) * 2 + target
            out[k, 0:W, :] = dot(rows_ref[:, lane(block)], normed, 0, 0).astype(BF16)
            gain = jnp.broadcast_to(gain_out[:, lane(block, 2 * W)], (GAINROWS, 2 * W))
            out[k, W : W + GAINROWS, :] = jnp.zeros((GAINROWS, INNER), BF16)
            out[k, W : W + GAINROWS, 0 : 2 * W] = gain.astype(BF16)
            flow.outgoing.copy(at, k).start()


def add_kernel(flow, own_term, other_term, own_ref, right_ref, left_ref, forth_ref, back_ref):
    for at, k in ((3, 2), (1, 1), (2, 3), (0, 0)):
        flow.arrive(k * STEP)
        total = (own_term[k].astype(F32) + other_term[k].astype(F32)).astype(BF16)
        if k == 2:
            forth_ref[...] = total[:, :D]
            back_ref[...] = total[:, D:]
            flow.outgoing.copy(4).start()
        else:
            (own_ref, right_ref, left_ref)[at][...] = total
        flow.outgoing.copy(at).start()


def relay_kernel(flow, right_in, left_in, forth_in, back_in, right_ref, left_ref):
    flow.arrive()
    right_ref[:, :D] = (right_in[:, :D].astype(F32) + forth_in[...].astype(F32)).astype(BF16)
    right_ref[:, D:] = right_in[:, D:]
    left_ref[:, :D] = left_in[:, :D]
    left_ref[:, D:] = (left_in[:, D:].astype(F32) + back_in[...].astype(F32)).astype(BF16)
    flow.leave()


def pair_kernel(
    flow, x_ref, grad_ref, b_ref, c_ref, row_ref, enter_ref,
    inner_ref, grad_c_ref, grad_b_ref, sum_ref,
):
    flow.arrive()
    b, c = b_ref[...], c_ref[...]
    scores = dot(b, c, 1, 1)
    causal = iota((T, T), 0) <= iota((T, T), 1)
    sum_ref[...] = jnp.zeros((T, T), F32)

    def step(pair, total):
        flow.arrive(pair)
        weights = []
        for h in (2 * pair, 2 * pair + 1):
            col = column(row_of(row_ref, h))
            differ = row_of(row_ref, h) - jnp.concatenate([col, col], axis=1)
            table = jnp.exp(jnp.where(causal, differ, FAR))
            grad = grad_ref[:, lane(h)]
            inner_ref[:, lane(h)] = dot((scores * table).astype(BF16), grad)
            weights.append(dot(x_ref[:, lane(h)], grad, 1, 1) * table)
        sum_ref[...] += weights[0] + weights[1]
        flow.leave(pair)
        start = (grad_ref[:, lane(pair, 2 * W)].astype(F32) * pair_starts(row_ref, pair)).astype(BF16)
        return total + dot(start, pair_state(enter_ref, pair), 1, 1)

    carried = lax.fori_loop(0, PAIRS, step, jnp.zeros((T, W), F32))
    weights = sum_ref[...].astype(BF16)
    grad_b_ref[...] = dot(weights, c)
    grad_c_ref[...] = (carried + dot(weights, b, 0, 0)).astype(BF16)
    flow.leave()


def sum_kernel(flow, *refs):
    *terms, out_ref, gain_ref = refs
    flow.arrive()
    total = terms[0][...].astype(F32)
    for term in terms[1:]:
        total = total + term[...].astype(F32)
    out_ref[...] = total[0:W, :].astype(BF16)
    gain_ref[...] = total[W : W + 8, 0 : 2 * W]
    flow.leave()


def last_kernel(
    flow, inner_ref, leave_ref, b_ref, x_ref, row_ref, grad_b_in, rate_ref, state_ref, enter_ref,
    grad_x_ref, grad_b_ref, decay_ref,
):
    flow.arrive()
    b = b_ref[...]

    def step(h, carry):
        flow.arrive(h)
        grad_b, rates, tail = carry
        cols = lane(h, 2 * W)
        leave = pair_state(leave_ref, h)
        keep, total = pair_ends(row_ref, h)
        grad_x = inner_ref[:, cols] + keep * dot(b, leave)
        grad_x_ref[:, cols] = grad_x.astype(BF16)
        flow.leave(h)
        x = x_ref[:, cols].astype(F32)
        rate = x * grad_x
        at = iota((T, W), 1)
        rates = rates - jnp.where(at == 2 * h, row_sum(rate[:, :W]), 0.0)
        rates = rates - jnp.where(at == 2 * h + 1, row_sum(rate[:, W:]), 0.0)
        state = pair_state(state_ref, h).astype(F32)
        later = jnp.exp(total) * pair_state(enter_ref, h).astype(F32) + state
        across = jnp.sum(later * leave.astype(F32), axis=0, keepdims=True)
        at = iota((W, 1), 0)
        tail = tail + jnp.where(at == 2 * h, row_sum(across[:, :W]), 0.0)
        tail = tail + jnp.where(at == 2 * h + 1, row_sum(across[:, W:]), 0.0)
        return grad_b + dot((x * keep).astype(BF16), leave, 1, 1), rates, tail

    start = (grad_b_in[...], rate_ref[...], jnp.zeros((W, 1), F32))
    grad_b, rates, tail = lax.fori_loop(0, H // 2, step, start)
    grad_b_ref[...] = grad_b.astype(BF16)
    lower = (iota((T, T), 0) >= iota((T, T), 1)).astype(F32)
    decay_ref[...] = (dot(rates, lower, 0, 0, precision=HI) + tail)[:H, :]
    flow.leave()


PAIRS = H // 2
CHUNKS = 4
STEP = PAIRS // CHUNKS


def chunked(array):
    return array.shape == (T, INNER) or len(array.shape) == 3 and array.shape[0] in (4, SEQ)


def part(ref, h):
    if len(ref.shape) == 2:
        return ref.at[:, lane(h, 2 * W * STEP)]
    count = ref.shape[0] // CHUNKS
    return ref.at[pl.ds(h * count, count)]


class Traffic:
    def __init__(self, sources, targets, sems):
        self.pairs = list(zip(sources, targets, range(len(sources))))
        self.sems = sems

    def copy(self, k, h=None):
        source, target, at = self.pairs[k]
        if h is None:
            return pltpu.make_async_copy(source, target, self.sems.at[at, 0])
        return pltpu.make_async_copy(part(source, h), part(target, h), self.sems.at[at, h])

    def where(self, pieces):
        return [k for k, (source, _, _) in enumerate(self.pairs) if chunked(source) == pieces]


class Flow:
    def __init__(self, incoming, outgoing):
        self.incoming, self.outgoing = incoming, outgoing

    def begin(self):
        for k in self.incoming.where(False):
            self.incoming.copy(k).start()
        for h in range(CHUNKS):
            for k in self.incoming.where(True):
                self.incoming.copy(k, h).start()

    def arrive(self, pair=None, last_first=False):
        if pair is None:
            for k in self.incoming.where(False):
                self.incoming.copy(k).wait()
            return

        @pl.when(lax.rem(pair, STEP) == (STEP - 1 if last_first else 0))
        def _():
            for k in self.incoming.where(True):
                self.incoming.copy(k, lax.div(pair, STEP)).wait()

    def leave(self, pair=None, last_first=False):
        if pair is None:
            for k in self.outgoing.where(False):
                self.outgoing.copy(k).start()
            return

        @pl.when(lax.rem(pair, STEP) == (0 if last_first else STEP - 1))
        def _():
            for k in self.outgoing.where(True):
                if self.outgoing.pairs[k][0].shape[0] != 4:
                    self.outgoing.copy(k, lax.div(pair, STEP)).start()

    def end(self):
        for k in self.outgoing.where(False):
            self.outgoing.copy(k).wait()
        for h in range(CHUNKS):
            for k in self.outgoing.where(True):
                self.outgoing.copy(k, h).wait()


def call(kernel, outs, args, scratch=(), smem=0, us=1.0, loose=(), after=(), own=False, near=()):
    scalars, arrays = args[:smem], args[smem:]
    held = sum(a.size * a.dtype.itemsize for a in (*arrays, *outs))
    room = held + sum(math.prod(s.shape) * 4 for s in scratch)
    spaces = [next((space for group, space in ((near, pltpu.VMEM), (loose, pl.ANY)) if any(a is b for b in group)), pltpu.HBM) for a in arrays]
    kept = [] if own else [a for a, space in zip(arrays, spaces) if space is not pltpu.VMEM]
    counts = (smem, len(arrays), len(after), len(outs), len(kept), len(outs), len(scratch))

    def run(*refs):
        groups = []
        for count in counts:
            groups.append(refs[:count])
            refs = refs[count:]
        numbers, sources, _, targets, copies, near_out, rest = groups
        far = [source for source, space in zip(sources, spaces) if space is not pltpu.VMEM]
        flow = Flow(Traffic(far, copies, refs[0]), Traffic(near_out, targets, refs[1]))
        if own:
            kernel(flow, *numbers, *sources, *near_out, *rest, refs[0])
        else:
            flow.begin()
            copies = list(copies)
            near_in = [s if space is pltpu.VMEM else copies.pop(0) for s, space in zip(sources, spaces)]
            kernel(flow, *numbers, *near_in, *near_out, *rest)
        flow.end()

    def tie(array, space):
        return array if space is pl.ANY else pltpu.with_memory_space_constraint(array, space)

    tied = [tie(a, space) for a, space in zip(arrays, spaces)]
    return pl.pallas_call(
        run,
        out_shape=[pltpu.HBM(out.shape, out.dtype) for out in outs],
        in_specs=[pl.BlockSpec(memory_space=pltpu.SMEM)] * smem
        + [pl.BlockSpec(memory_space=space) for space in spaces]
        + [pl.BlockSpec(memory_space=pl.ANY)] * len(after),
        out_specs=[pl.BlockSpec(memory_space=pltpu.HBM)] * len(outs),
        scratch_shapes=[
            *(pltpu.VMEM(a.shape, a.dtype) for a in (*kept, *outs)),
            *scratch,
            pltpu.SemaphoreType.DMA((len(arrays), CHUNKS)),
            pltpu.SemaphoreType.DMA((len(outs), CHUNKS)),
        ],
        compiler_params=pltpu.CompilerParams(vmem_limit_bytes=room + 6 * 2**20),
        cost_estimate=pl.CostEstimate(flops=int(us * 1.1e9), bytes_accessed=held, transcendentals=0),
    )(*scalars, *tied, *(pltpu.with_memory_space_constraint(a, pltpu.HBM) for a in after))


def shaped(shape, dtype=F32):
    return jax.ShapeDtypeStruct(shape, dtype)


def shift(value, axis, by):
    size = lax.axis_size(axis)
    return lax.ppermute(value, axis, [(i, (i + by) % size) for i in range(size)])


def shifts(values, axis):
    return [value if k == 0 else shift(value, axis, k) for k, value in enumerate(values)]


def exchange(value, axes=SEQ_AXES):
    return lax.all_to_all(value, axes, 0, 0, tiled=True)


def body(ssm, gate, state_in, state_out, log_decay, gain, out_weight, grad_rows):
    x, b, c = ssm[0], state_in[0], state_out[0]
    gate, grad_rows, gain_row = gate[0], grad_rows[0], gain[None]
    at = jnp.stack([lax.axis_index(name) for name in ("x", "c", "y")]).astype(jnp.int32)
    wide = shaped((T, INNER))
    wide_bf = shaped((T, INNER), BF16)
    states = shaped((SEQ, HALF, W), BF16)

    send, row = call(
        state_kernel,
        [shaped((SEQ, HALF + EXTRA, W), BF16), shaped((H, T))],
        [x, b, log_decay[0].T],
        us=0.1,
    )
    got = exchange(send)

    own = exchange(jnp.broadcast_to(out_weight.T, (8, 8, D)), "z").reshape(HALF, D)
    [inner] = call(inner_kernel, [wide_bf], [x, b, c, row], us=0.3)
    slices = shifts([own] * 4, "y")
    [ordered] = call(
        order_kernel, [shaped((T, D), BF16)], [at, *slices], smem=1, us=0.1, loose=slices, own=True, after=[inner]
    )
    pieces = shifts([ordered] * 4, "x")
    pieces += [shift(piece, "c", 1) for piece in pieces]

    enter_part, factor = call(
        forward_scan_kernel, [states, shaped((SEQ, W))], [got], us=0.1, loose=[got]
    )
    enter = exchange(enter_part)
    [grad_normed] = call(
        normed_grad_kernel,
        [wide_bf],
        [at, grad_rows, *pieces],
        scratch=[pltpu.VMEM((T, D), BF16), pltpu.VMEM((4, T, D), BF16)],
        own=True,
        smem=1,
        us=1.0,
        loose=[pieces[1], pieces[3], pieces[4]],
        near=[pieces[k] for k in range(8) if k not in FAR_PIECES],
    )
    grad_gate, grad_y, grad_send, rate, own_term, other_term = call(
        norm_kernel,
        [wide_bf, wide_bf, states, shaped((T, W)), *[shaped((4, W + GAINROWS, INNER), BF16)] * 2],
        [at, inner, grad_normed, gate, enter, c, row, gain_row, grad_rows],
        scratch=[
            pltpu.VMEM((T, INNER), F32),
            pltpu.VMEM((T, INNER), F32),
            pltpu.VMEM((T, INNER), BF16),
            pltpu.VMEM((1, INNER), F32),
        ],
        smem=1,
        us=0.3,
        loose=[enter],
    )
    grad_got = exchange(grad_send)
    other_term = shift(other_term, "c", 1)
    block = shaped((W + GAINROWS, INNER), BF16)
    half = shaped((W + GAINROWS, D), BF16)
    kept, right, left, forth, back = call(
        add_kernel, [block, block, block, half, half], [own_term, other_term], us=3.7, loose=[other_term]
    )
    forth, back = shift(forth, "x", 1), shift(back, "x", -1)
    right, left = call(
        relay_kernel, [block, block], [right, left, forth, back], us=2.8, near=[forth, back]
    )
    [leave_part] = call(
        backward_scan_kernel, [states], [grad_got, factor], us=2.0, loose=[grad_got], after=[right]
    )
    leave = exchange(leave_part)
    right, left = shift(right, "x", 1), shift(left, "x", -1)
    quarter, gains = call(
        sum_kernel,
        [shaped((W, INNER), BF16), shaped((8, 2 * W))],
        [kept, right, left],
        us=2.6,
        near=[right, left],
    )
    grad_inner, grad_state_out, grad_b = call(
        pair_kernel,
        [wide, shaped((T, W), BF16), shaped((T, W))],
        [x, grad_y, b, c, row, enter],
        scratch=[pltpu.VMEM((T, T), F32)],
        us=5.8,
        loose=[enter],
        after=[leave_part],
    )
    rows = quarter.reshape(SEQ, HALF, W)
    gains = jnp.pad(gains[0].astype(BF16).reshape(SEQ, 1, 8), ((0, 0), (0, 7), (0, W - 8)))
    final = jnp.sum(exchange(jnp.concatenate([rows, gains], axis=1)).astype(F32), axis=0)
    grad_input, grad_state_in, grad_log_decay = call(
        last_kernel,
        [wide_bf, shaped((T, W), BF16), shaped((H, T))],
        [grad_inner, leave, b, x, row, grad_b, rate, send, enter],
        us=5.5,
        loose=[leave, enter],
    )
    return (
        grad_input[None],
        grad_gate[None],
        grad_state_in[None],
        grad_state_out[None],
        grad_log_decay.T[None],
        final[:HALF].reshape(4, INNER),
        final[HALF, :8],
    )


def solution(mesh):
    split = Mesh(mesh.devices.reshape(4, 2, 4, 8), ("x", "c", "y", "z"))
    shower, seq = ("x", "c"), ("y", "z")
    rows = P(shower, seq, None)
    every = (*shower, *seq)
    return jax.shard_map(
        body,
        mesh=split,
        in_specs=(rows, rows, rows, rows, rows, P(), P(None, every), rows),
        out_specs=(rows, rows, rows, rows, rows, P(every, None), P(every)),
        check_vma=False,
    )
```

```python
import math

import jax
import jax.numpy as jnp
from jax import lax
from jax.experimental import pallas as pl
from jax.experimental.pallas import tpu as pltpu
from jax.sharding import Mesh
from jax.sharding import PartitionSpec as P

F32, BF16 = jnp.float32, jnp.bfloat16
T = 256
H = 16
W = 128
INNER = H * W
D = 1024
SEQ = 32
HALF = 64
EXTRA = 16
GAINROWS = 16
SEQ_AXES = ("y", "z")
FAR = -1e30
HI = lax.Precision.HIGHEST


def lane(h, width=W):
    return pl.ds(pl.multiple_of(h * width, width), width)


def dot(a, b, ca=1, cb=0, precision=None):
    return lax.dot_general(
        a, b, (((ca,), (cb,)), ((), ())), precision=precision, preferred_element_type=F32
    )


def iota(shape, axis):
    return lax.broadcasted_iota(jnp.int32, shape, axis)


def row_sum(a):
    return jnp.sum(a, axis=1, keepdims=True)


def column(row):
    return jnp.broadcast_to(row, (W, T)).T


def row_of(ref, h):
    return ref[pl.ds(h, 1), :]


def pair_starts(ref, h):
    return jnp.concatenate([column(jnp.exp(row_of(ref, 2 * h + k))) for k in range(2)], axis=1)


def pair_ends(ref, h):
    rows = [row_of(ref, 2 * h + k) for k in range(2)]
    keep = jnp.concatenate([column(jnp.exp(row[:, T - 1 :] - row)) for row in rows], axis=1)
    total = jnp.concatenate([jnp.broadcast_to(row[:, T - 1 :], (1, W)) for row in rows], axis=1)
    return keep, total


def pair_state(ref, h):
    blocks = ref[pl.ds(4 * h, 4), 0:HALF, :]
    first = blocks[0:2].reshape(W, W)
    second = blocks[2:4].reshape(W, W)
    return jnp.concatenate([first, second], axis=1)


def split_state(ref, h, value):
    ref[pl.ds(4 * h, 2), 0:HALF, :] = value[:, :W].reshape(2, HALF, W)
    ref[pl.ds(4 * h + 2, 2), 0:HALF, :] = value[:, W:].reshape(2, HALF, W)


def state_kernel(flow, x_ref, b_ref, decay_ref, send_ref, row_ref):
    tri = (iota((T, T), 0) >= iota((T, T), 1)).astype(F32)
    flow.arrive()
    decay = decay_ref[...]
    row_ref[...] = dot(decay, tri, 1, 1, precision=HI)
    flow.leave()
    b = b_ref[...]

    @pl.loop(0, H // 2)
    def _(h):
        flow.arrive(h)
        keep, total = pair_ends(row_ref, h)
        cols = lane(h, 2 * W)
        x_end = (x_ref[:, cols].astype(F32) * keep).astype(BF16)
        split_state(send_ref, h, dot(b, x_end, 0, 0).astype(BF16))
        high = total.astype(BF16).astype(F32)
        middle = (total - high).astype(BF16).astype(F32)
        low = total - high - middle
        at = iota((EXTRA, 2 * W), 0)
        rows = jnp.where(at == 0, high, jnp.where(at == 1, middle, jnp.where(at == 2, low, 0.0)))
        rows = rows.astype(BF16)
        for k in range(4):
            half = rows[:, :W] if k < 2 else rows[:, W:]
            send_ref[4 * h + k, HALF : HALF + EXTRA, :] = half
        flow.leave(h)


def forward_scan_kernel(flow, got_ref, out_ref, factor_ref):
    group = SEQ // PAIRS

    def step(h, carry):
        flow.arrive(h)
        for k in range(group):
            j = h * group + k
            out_ref[j] = carry.astype(BF16)
            tail = got_ref[j, HALF : HALF + EXTRA, :].astype(F32)
            factor = jnp.exp(jnp.sum(tail, axis=0, keepdims=True))
            factor_ref[pl.ds(j, 1), :] = factor
            carry = factor * carry + got_ref[j, 0:HALF, :].astype(F32)
        flow.leave(h)
        return carry

    lax.fori_loop(0, PAIRS, step, jnp.zeros((HALF, W), F32))
    flow.leave()


def backward_scan_kernel(flow, got_ref, factor_ref, out_ref):
    group = SEQ // PAIRS
    flow.arrive()

    def step(i, carry):
        h = PAIRS - 1 - i
        flow.arrive(h, True)
        for k in range(group - 1, -1, -1):
            j = h * group + k
            out_ref[j] = carry.astype(BF16)
            carry = factor_ref[pl.ds(j, 1), :] * carry + got_ref[j].astype(F32)
        flow.leave(h, True)
        return carry

    lax.fori_loop(0, PAIRS, step, jnp.zeros((HALF, W), F32))


def inner_kernel(flow, x_ref, b_ref, c_ref, row_ref, inner_ref):
    flow.arrive()
    scores = dot(c_ref[...], b_ref[...], 1, 1)
    causal = iota((T, T), 0) >= iota((T, T), 1)

    @pl.loop(0, PAIRS)
    def _(pair):
        flow.arrive(pair)
        for h in (2 * pair, 2 * pair + 1):
            col = column(row_of(row_ref, h))
            differ = jnp.concatenate([col, col], axis=1) - row_of(row_ref, h)
            kernel = (scores * jnp.exp(jnp.where(causal, differ, FAR))).astype(BF16)
            inner_ref[:, lane(h)] = dot(kernel, x_ref[:, lane(h)]).astype(BF16)
        flow.leave(pair)


def order_kernel(flow, at_ref, *refs):
    pieces, (_, sems) = refs[:4], refs[4:]
    target = flow.outgoing.pairs.pop()[1]
    copies = []
    for k, piece in enumerate(pieces):
        rows = pl.multiple_of(lax.rem(at_ref[2] + 4 - k, 4) * HALF, HALF)
        copies.append(pltpu.make_async_copy(piece, target.at[pl.ds(rows, HALF), :], sems.at[k, 0]))
        copies[k].start()
    for copy in copies:
        copy.wait()


def norm_kernel(flow, at_ref, inner_ref, gate_ref, enter_ref, c_ref, row_ref, gain_ref, rows_ref, *refs):
    pieces, refs = refs[:8], refs[8:]
    gate_out, grad_out, send_ref, rate_out, own_ref, other_ref = refs[:6]
    y_ref, sig_ref, normed_out, gain_out, gn_ref, weight_ref, sems = refs[6:]
    x, core = at_ref[0], at_ref[1]
    copies = [pltpu.make_async_copy(pieces[k], weight_ref.at[k], sems.at[k]) for k in range(8)]
    for copy in copies:
        copy.start()
    flow.arrive()
    c = c_ref[...]

    def first(h, squares):
        flow.arrive(h)
        cols = lane(h, 2 * W)
        keep = pair_starts(row_ref, h)
        y = inner_ref[:, cols].astype(F32) + keep * dot(c, pair_state(enter_ref, h))
        gate = gate_ref[:, cols].astype(F32)
        sig = 0.5 * jnp.tanh(0.5 * gate) + 0.5
        u = y * (gate * sig)
        y_ref[:, cols] = y
        sig_ref[:, cols] = sig
        squared = u * u
        return squares + squared[:, :W] + squared[:, W:]

    def second(h, mixed):
        cols = lane(h, 2 * W)
        other = jnp.abs(lax.rem(h, 2) - core)
        slot = 4 * other + lax.rem(x + 4 - lax.div(h, 2), 4)
        gn = dot(rows_ref[...], weight_ref[slot], 1, 1)
        gn_ref[:, cols] = gn
        u = y_ref[:, cols] * (gate_ref[:, cols].astype(F32) * sig_ref[:, cols])
        both = gain_ref[:, cols] * gn * u
        return mixed + both[:, :W] + both[:, W:]

    zero = jnp.zeros((T, W), F32)
    squares = lax.fori_loop(0, H // 2, first, zero)
    for copy in copies:
        copy.wait()
    mixed = lax.fori_loop(0, H // 2, second, zero)
    rstd = lax.rsqrt(row_sum(squares) / INNER + 1e-5)
    pull = rstd * rstd * rstd * (row_sum(mixed) / INNER)
    rate_out[...] = zero

    @pl.loop(0, H // 2)
    def _(h):
        cols = lane(h, 2 * W)
        y, sig, gn = y_ref[:, cols], sig_ref[:, cols], gn_ref[:, cols]
        gain = gain_ref[:, cols]
        gate = gate_ref[:, cols].astype(F32)
        active = gate * sig
        u = y * active
        normal = u * rstd
        grad_u = rstd * (gain * gn) - u * pull
        grad_y = grad_u * active
        gate_out[:, cols] = (grad_u * y * (sig + active * (1.0 - sig))).astype(BF16)
        normed_out[:, cols] = (normal * gain).astype(BF16)
        gain_out[:, cols] = jnp.sum(gn * normal, axis=0, keepdims=True)
        grad_out[:, cols] = grad_y.astype(BF16)
        start = (grad_y * pair_starts(row_ref, h)).astype(BF16)
        rate = grad_y * y
        at = iota((T, W), 1)
        rates = rate_out[...]
        rates = jnp.where(at == 2 * h, row_sum(rate[:, :W]), rates)
        rate_out[...] = jnp.where(at == 2 * h + 1, row_sum(rate[:, W:]), rates)
        split_state(send_ref, h, dot(c, start, 0, 0).astype(BF16))
        flow.leave(h)

    flow.leave()
    normed = normed_out[...]
    for at, out, target in ((5, other_ref, 1 - core), (4, own_ref, core)):
        for k in range(4):
            block = lax.rem(x + k, 4) * 2 + target
            out[k, 0:W, :] = dot(rows_ref[:, lane(block)], normed, 0, 0).astype(BF16)
            gain = jnp.broadcast_to(gain_out[:, lane(block, 2 * W)], (GAINROWS, 2 * W))
            out[k, W : W + GAINROWS, :] = jnp.zeros((GAINROWS, INNER), BF16)
            out[k, W : W + GAINROWS, 0 : 2 * W] = gain.astype(BF16)
            flow.outgoing.copy(at, k).start()


def add_kernel(flow, own_term, other_term, own_ref, right_ref, left_ref, forth_ref, back_ref):
    for at, k in ((3, 2), (1, 1), (2, 3), (0, 0)):
        flow.arrive(k * STEP)
        total = (own_term[k].astype(F32) + other_term[k].astype(F32)).astype(BF16)
        if k == 2:
            forth_ref[...] = total[:, :D]
            back_ref[...] = total[:, D:]
            flow.outgoing.copy(4).start()
        else:
            (own_ref, right_ref, left_ref)[at][...] = total
        flow.outgoing.copy(at).start()


def relay_kernel(flow, right_in, left_in, forth_in, back_in, right_ref, left_ref):
    flow.arrive()
    right_ref[:, :D] = (right_in[:, :D].astype(F32) + forth_in[...].astype(F32)).astype(BF16)
    right_ref[:, D:] = right_in[:, D:]
    left_ref[:, :D] = left_in[:, :D]
    left_ref[:, D:] = (left_in[:, D:].astype(F32) + back_in[...].astype(F32)).astype(BF16)
    flow.leave()


def pair_kernel(
    flow, x_ref, grad_ref, b_ref, c_ref, row_ref, enter_ref,
    inner_ref, grad_c_ref, grad_b_ref, sum_ref,
):
    flow.arrive()
    b, c = b_ref[...], c_ref[...]
    scores = dot(b, c, 1, 1)
    causal = iota((T, T), 0) <= iota((T, T), 1)
    sum_ref[...] = jnp.zeros((T, T), F32)

    def step(pair, total):
        flow.arrive(pair)
        weights = []
        for h in (2 * pair, 2 * pair + 1):
            col = column(row_of(row_ref, h))
            differ = row_of(row_ref, h) - jnp.concatenate([col, col], axis=1)
            table = jnp.exp(jnp.where(causal, differ, FAR))
            grad = grad_ref[:, lane(h)]
            inner_ref[:, lane(h)] = dot((scores * table).astype(BF16), grad)
            weights.append(dot(x_ref[:, lane(h)], grad, 1, 1) * table)
        sum_ref[...] += weights[0] + weights[1]
        flow.leave(pair)
        start = (grad_ref[:, lane(pair, 2 * W)].astype(F32) * pair_starts(row_ref, pair)).astype(BF16)
        return total + dot(start, pair_state(enter_ref, pair), 1, 1)

    carried = lax.fori_loop(0, PAIRS, step, jnp.zeros((T, W), F32))
    weights = sum_ref[...].astype(BF16)
    grad_b_ref[...] = dot(weights, c)
    grad_c_ref[...] = (carried + dot(weights, b, 0, 0)).astype(BF16)
    flow.leave()


def sum_kernel(flow, *refs):
    *terms, out_ref, gain_ref = refs
    flow.arrive()
    total = terms[0][...].astype(F32)
    for term in terms[1:]:
        total = total + term[...].astype(F32)
    out_ref[...] = total[0:W, :].astype(BF16)
    gain_ref[...] = total[W : W + 8, 0 : 2 * W]
    flow.leave()


def last_kernel(
    flow, inner_ref, leave_ref, b_ref, x_ref, row_ref, grad_b_in, rate_ref, state_ref, enter_ref,
    grad_x_ref, grad_b_ref, decay_ref,
):
    flow.arrive()
    b = b_ref[...]

    def step(h, carry):
        flow.arrive(h)
        grad_b, rates, tail = carry
        cols = lane(h, 2 * W)
        leave = pair_state(leave_ref, h)
        keep, total = pair_ends(row_ref, h)
        grad_x = inner_ref[:, cols] + keep * dot(b, leave)
        grad_x_ref[:, cols] = grad_x.astype(BF16)
        flow.leave(h)
        x = x_ref[:, cols].astype(F32)
        rate = x * grad_x
        at = iota((T, W), 1)
        rates = rates - jnp.where(at == 2 * h, row_sum(rate[:, :W]), 0.0)
        rates = rates - jnp.where(at == 2 * h + 1, row_sum(rate[:, W:]), 0.0)
        state = pair_state(state_ref, h).astype(F32)
        later = jnp.exp(total) * pair_state(enter_ref, h).astype(F32) + state
        across = jnp.sum(later * leave.astype(F32), axis=0, keepdims=True)
        at = iota((W, 1), 0)
        tail = tail + jnp.where(at == 2 * h, row_sum(across[:, :W]), 0.0)
        tail = tail + jnp.where(at == 2 * h + 1, row_sum(across[:, W:]), 0.0)
        return grad_b + dot((x * keep).astype(BF16), leave, 1, 1), rates, tail

    start = (grad_b_in[...], rate_ref[...], jnp.zeros((W, 1), F32))
    grad_b, rates, tail = lax.fori_loop(0, H // 2, step, start)
    grad_b_ref[...] = grad_b.astype(BF16)
    lower = (iota((T, T), 0) >= iota((T, T), 1)).astype(F32)
    decay_ref[...] = (dot(rates, lower, 0, 0, precision=HI) + tail)[:H, :]
    flow.leave()


PAIRS = H // 2
CHUNKS = 4
STEP = PAIRS // CHUNKS


def chunked(array):
    return array.shape == (T, INNER) or len(array.shape) == 3 and array.shape[0] in (4, SEQ)


def part(ref, h):
    if len(ref.shape) == 2:
        return ref.at[:, lane(h, 2 * W * STEP)]
    count = ref.shape[0] // CHUNKS
    return ref.at[pl.ds(h * count, count)]


class Traffic:
    def __init__(self, sources, targets, sems):
        self.pairs = list(zip(sources, targets, range(len(sources))))
        self.sems = sems

    def copy(self, k, h=None):
        source, target, at = self.pairs[k]
        if h is None:
            return pltpu.make_async_copy(source, target, self.sems.at[at, 0])
        return pltpu.make_async_copy(part(source, h), part(target, h), self.sems.at[at, h])

    def where(self, pieces):
        return [k for k, (source, _, _) in enumerate(self.pairs) if chunked(source) == pieces]


class Flow:
    def __init__(self, incoming, outgoing):
        self.incoming, self.outgoing = incoming, outgoing

    def begin(self):
        for k in self.incoming.where(False):
            self.incoming.copy(k).start()
        for h in range(CHUNKS):
            for k in self.incoming.where(True):
                self.incoming.copy(k, h).start()

    def arrive(self, pair=None, last_first=False):
        if pair is None:
            for k in self.incoming.where(False):
                self.incoming.copy(k).wait()
            return

        @pl.when(lax.rem(pair, STEP) == (STEP - 1 if last_first else 0))
        def _():
            for k in self.incoming.where(True):
                self.incoming.copy(k, lax.div(pair, STEP)).wait()

    def leave(self, pair=None, last_first=False):
        if pair is None:
            for k in self.outgoing.where(False):
                self.outgoing.copy(k).start()
            return

        @pl.when(lax.rem(pair, STEP) == (0 if last_first else STEP - 1))
        def _():
            for k in self.outgoing.where(True):
                if self.outgoing.pairs[k][0].shape[0] != 4:
                    self.outgoing.copy(k, lax.div(pair, STEP)).start()

    def end(self):
        for k in self.outgoing.where(False):
            self.outgoing.copy(k).wait()
        for h in range(CHUNKS):
            for k in self.outgoing.where(True):
                self.outgoing.copy(k, h).wait()


def call(kernel, outs, args, scratch=(), smem=0, us=1.0, loose=(), after=(), own=False, near=(), raw=()):
    scalars, arrays = args[:smem], args[smem:]
    held = sum(a.size * a.dtype.itemsize for a in (*arrays, *outs))
    room = held + sum(math.prod(s.shape) * 4 for s in scratch)
    spaces = [next((space for group, space in ((near, pltpu.VMEM), (loose, pl.ANY)) if any(a is b for b in group)), pltpu.HBM) for a in arrays]
    direct = [space is pltpu.VMEM or any(a is b for b in raw) for a, space in zip(arrays, spaces)]
    kept = [] if own else [a for a, skip in zip(arrays, direct) if not skip]
    counts = (smem, len(arrays), len(after), len(outs), len(kept), len(outs), len(scratch))

    def run(*refs):
        groups = []
        for count in counts:
            groups.append(refs[:count])
            refs = refs[count:]
        numbers, sources, _, targets, copies, near_out, rest = groups
        far = [source for source, skip in zip(sources, direct) if not skip]
        flow = Flow(Traffic(far, copies, refs[0]), Traffic(near_out, targets, refs[1]))
        if own:
            kernel(flow, *numbers, *sources, *near_out, *rest, refs[0])
        else:
            flow.begin()
            copies = list(copies)
            near_in = [source if skip else copies.pop(0) for source, skip in zip(sources, direct)]
            kernel(flow, *numbers, *near_in, *near_out, *rest)
        flow.end()

    def tie(array, space):
        return array if space is pl.ANY else pltpu.with_memory_space_constraint(array, space)

    tied = [tie(a, space) for a, space in zip(arrays, spaces)]
    return pl.pallas_call(
        run,
        out_shape=[pltpu.HBM(out.shape, out.dtype) for out in outs],
        in_specs=[pl.BlockSpec(memory_space=pltpu.SMEM)] * smem
        + [pl.BlockSpec(memory_space=space) for space in spaces]
        + [pl.BlockSpec(memory_space=pl.ANY)] * len(after),
        out_specs=[pl.BlockSpec(memory_space=pltpu.HBM)] * len(outs),
        scratch_shapes=[
            *(pltpu.VMEM(a.shape, a.dtype) for a in (*kept, *outs)),
            *scratch,
            pltpu.SemaphoreType.DMA((len(arrays), CHUNKS)),
            pltpu.SemaphoreType.DMA((len(outs), CHUNKS)),
        ],
        compiler_params=pltpu.CompilerParams(vmem_limit_bytes=room + 6 * 2**20),
        cost_estimate=pl.CostEstimate(flops=int(us * 1.1e9), bytes_accessed=held, transcendentals=0),
    )(*scalars, *tied, *(pltpu.with_memory_space_constraint(a, pltpu.HBM) for a in after))


def shaped(shape, dtype=F32):
    return jax.ShapeDtypeStruct(shape, dtype)


def shift(value, axis, by):
    size = lax.axis_size(axis)
    return lax.ppermute(value, axis, [(i, (i + by) % size) for i in range(size)])


def shifts(values, axis):
    return [value if k == 0 else shift(value, axis, k) for k, value in enumerate(values)]


def exchange(value, axes=SEQ_AXES):
    return lax.all_to_all(value, axes, 0, 0, tiled=True)


def body(ssm, gate, state_in, state_out, log_decay, gain, out_weight, grad_rows):
    x, b, c = ssm[0], state_in[0], state_out[0]
    gate, grad_rows, gain_row = gate[0], grad_rows[0], gain[None]
    at = jnp.stack([lax.axis_index(name) for name in ("x", "c", "y")]).astype(jnp.int32)
    wide = shaped((T, INNER))
    wide_bf = shaped((T, INNER), BF16)
    states = shaped((SEQ, HALF, W), BF16)

    send, row = call(
        state_kernel,
        [shaped((SEQ, HALF + EXTRA, W), BF16), shaped((H, T))],
        [x, b, log_decay[0].T],
        us=0.1,
    )
    got = exchange(send)

    own = exchange(jnp.broadcast_to(out_weight.T, (8, 8, D)), "z").reshape(HALF, D)
    [inner] = call(inner_kernel, [wide_bf], [x, b, c, row], us=0.3)
    slices = shifts([own] * 4, "y")
    [ordered] = call(
        order_kernel, [shaped((T, D), BF16)], [at, *slices], smem=1, us=0.1, loose=slices, own=True, after=[inner]
    )
    pieces = shifts([ordered] * 4, "x")
    pieces += [shift(piece, "c", 1) for piece in pieces]

    enter_part, factor = call(
        forward_scan_kernel, [states, shaped((SEQ, W))], [got], us=0.1, loose=[got]
    )
    enter = exchange(enter_part)
    grad_gate, grad_y, grad_send, rate, own_term, other_term = call(
        norm_kernel,
        [wide_bf, wide_bf, states, shaped((T, W)), *[shaped((4, W + GAINROWS, INNER), BF16)] * 2],
        [at, inner, gate, enter, c, row, gain_row, grad_rows, *pieces],
        scratch=[
            pltpu.VMEM((T, INNER), F32),
            pltpu.VMEM((T, INNER), F32),
            pltpu.VMEM((T, INNER), BF16),
            pltpu.VMEM((1, INNER), F32),
            pltpu.VMEM((T, INNER), F32),
            pltpu.VMEM((8, T, D), BF16),
            pltpu.SemaphoreType.DMA((8,)),
        ],
        smem=1,
        us=1.3,
        loose=[enter, *pieces[1:5], pieces[7]],
        raw=pieces,
    )
    grad_got = exchange(grad_send)
    other_term = shift(other_term, "c", 1)
    block = shaped((W + GAINROWS, INNER), BF16)
    half = shaped((W + GAINROWS, D), BF16)
    kept, right, left, forth, back = call(
        add_kernel, [block, block, block, half, half], [own_term, other_term], us=3.7, loose=[other_term]
    )
    forth, back = shift(forth, "x", 1), shift(back, "x", -1)
    right, left = call(
        relay_kernel, [block, block], [right, left, forth, back], us=2.8, near=[forth, back]
    )
    [leave_part] = call(
        backward_scan_kernel, [states], [grad_got, factor], us=2.0, loose=[grad_got], after=[right]
    )
    leave = exchange(leave_part)
    right, left = shift(right, "x", 1), shift(left, "x", -1)
    quarter, gains = call(
        sum_kernel,
        [shaped((W, INNER), BF16), shaped((8, 2 * W))],
        [kept, right, left],
        us=2.6,
        near=[right, left],
    )
    grad_inner, grad_state_out, grad_b = call(
        pair_kernel,
        [wide, shaped((T, W), BF16), shaped((T, W))],
        [x, grad_y, b, c, row, enter],
        scratch=[pltpu.VMEM((T, T), F32)],
        us=5.8,
        loose=[enter],
        after=[leave_part],
    )
    rows = quarter.reshape(SEQ, HALF, W)
    gains = jnp.pad(gains[0].astype(BF16).reshape(SEQ, 1, 8), ((0, 0), (0, 7), (0, W - 8)))
    final = jnp.sum(exchange(jnp.concatenate([rows, gains], axis=1)).astype(F32), axis=0)
    grad_input, grad_state_in, grad_log_decay = call(
        last_kernel,
        [wide_bf, shaped((T, W), BF16), shaped((H, T))],
        [grad_inner, leave, b, x, row, grad_b, rate, send, enter],
        us=5.5,
        loose=[leave, enter],
    )
    return (
        grad_input[None],
        grad_gate[None],
        grad_state_in[None],
        grad_state_out[None],
        grad_log_decay.T[None],
        final[:HALF].reshape(4, INNER),
        final[HALF, :8],
    )


def solution(mesh):
    split = Mesh(mesh.devices.reshape(4, 2, 4, 8), ("x", "c", "y", "z"))
    shower, seq = ("x", "c"), ("y", "z")
    rows = P(shower, seq, None)
    every = (*shower, *seq)
    return jax.shard_map(
        body,
        mesh=split,
        in_specs=(rows, rows, rows, rows, rows, P(), P(None, every), rows),
        out_specs=(rows, rows, rows, rows, rows, P(every, None), P(every)),
        check_vma=False,
    )
```

```python
import math

import jax
import jax.numpy as jnp
from jax import lax
from jax.experimental import pallas as pl
from jax.experimental.pallas import tpu as pltpu
from jax.sharding import Mesh
from jax.sharding import PartitionSpec as P

F32, BF16 = jnp.float32, jnp.bfloat16
T = 256
H = 16
W = 128
INNER = H * W
D = 1024
SEQ = 32
HALF = 64
EXTRA = 16
GAINROWS = 16
SEQ_AXES = ("y", "z")
FAR = -1e30
HI = lax.Precision.HIGHEST


def lane(h, width=W):
    return pl.ds(pl.multiple_of(h * width, width), width)


def dot(a, b, ca=1, cb=0, precision=None):
    return lax.dot_general(
        a, b, (((ca,), (cb,)), ((), ())), precision=precision, preferred_element_type=F32
    )


def iota(shape, axis):
    return lax.broadcasted_iota(jnp.int32, shape, axis)


def row_sum(a):
    return jnp.sum(a, axis=1, keepdims=True)


def column(row):
    return jnp.broadcast_to(row, (W, T)).T


def row_of(ref, h):
    return ref[pl.ds(h, 1), :]


def pair_starts(ref, h):
    return jnp.concatenate([column(jnp.exp(row_of(ref, 2 * h + k))) for k in range(2)], axis=1)


def pair_ends(ref, h):
    rows = [row_of(ref, 2 * h + k) for k in range(2)]
    keep = jnp.concatenate([column(jnp.exp(row[:, T - 1 :] - row)) for row in rows], axis=1)
    total = jnp.concatenate([jnp.broadcast_to(row[:, T - 1 :], (1, W)) for row in rows], axis=1)
    return keep, total


def pair_state(ref, h):
    blocks = ref[pl.ds(4 * h, 4), 0:HALF, :]
    first = blocks[0:2].reshape(W, W)
    second = blocks[2:4].reshape(W, W)
    return jnp.concatenate([first, second], axis=1)


def split_state(ref, h, value):
    ref[pl.ds(4 * h, 2), 0:HALF, :] = value[:, :W].reshape(2, HALF, W)
    ref[pl.ds(4 * h + 2, 2), 0:HALF, :] = value[:, W:].reshape(2, HALF, W)


def state_kernel(flow, x_ref, b_ref, decay_ref, send_ref, row_ref):
    tri = (iota((T, T), 0) >= iota((T, T), 1)).astype(F32)
    flow.arrive()
    decay = decay_ref[...]
    row_ref[...] = dot(decay, tri, 1, 1, precision=HI)
    flow.leave()
    b = b_ref[...]

    @pl.loop(0, H // 2)
    def _(h):
        flow.arrive(h)
        keep, total = pair_ends(row_ref, h)
        cols = lane(h, 2 * W)
        x_end = (x_ref[:, cols].astype(F32) * keep).astype(BF16)
        split_state(send_ref, h, dot(b, x_end, 0, 0).astype(BF16))
        high = total.astype(BF16).astype(F32)
        middle = (total - high).astype(BF16).astype(F32)
        low = total - high - middle
        at = iota((EXTRA, 2 * W), 0)
        rows = jnp.where(at == 0, high, jnp.where(at == 1, middle, jnp.where(at == 2, low, 0.0)))
        rows = rows.astype(BF16)
        for k in range(4):
            half = rows[:, :W] if k < 2 else rows[:, W:]
            send_ref[4 * h + k, HALF : HALF + EXTRA, :] = half
        flow.leave(h)


def forward_scan_kernel(flow, got_ref, out_ref, factor_ref):
    group = SEQ // PAIRS

    def step(h, carry):
        flow.arrive(h)
        for k in range(group):
            j = h * group + k
            out_ref[j] = carry.astype(BF16)
            tail = got_ref[j, HALF : HALF + EXTRA, :].astype(F32)
            factor = jnp.exp(jnp.sum(tail, axis=0, keepdims=True))
            factor_ref[pl.ds(j, 1), :] = factor
            carry = factor * carry + got_ref[j, 0:HALF, :].astype(F32)
        flow.leave(h)
        return carry

    lax.fori_loop(0, PAIRS, step, jnp.zeros((HALF, W), F32))
    flow.leave()


def backward_scan_kernel(flow, got_ref, factor_ref, out_ref):
    group = SEQ // PAIRS
    flow.arrive()

    def step(i, carry):
        h = PAIRS - 1 - i
        flow.arrive(h, True)
        for k in range(group - 1, -1, -1):
            j = h * group + k
            out_ref[j] = carry.astype(BF16)
            carry = factor_ref[pl.ds(j, 1), :] * carry + got_ref[j].astype(F32)
        flow.leave(h, True)
        return carry

    lax.fori_loop(0, PAIRS, step, jnp.zeros((HALF, W), F32))


def inner_kernel(flow, x_ref, b_ref, c_ref, row_ref, inner_ref):
    flow.arrive()
    scores = dot(c_ref[...], b_ref[...], 1, 1)
    causal = iota((T, T), 0) >= iota((T, T), 1)

    @pl.loop(0, PAIRS)
    def _(pair):
        flow.arrive(pair)
        for h in (2 * pair, 2 * pair + 1):
            col = column(row_of(row_ref, h))
            differ = jnp.concatenate([col, col], axis=1) - row_of(row_ref, h)
            kernel = (scores * jnp.exp(jnp.where(causal, differ, FAR))).astype(BF16)
            inner_ref[:, lane(h)] = dot(kernel, x_ref[:, lane(h)]).astype(BF16)
        flow.leave(pair)


def order_kernel(flow, at_ref, *refs):
    pieces, (_, sems) = refs[:4], refs[4:]
    target = flow.outgoing.pairs.pop()[1]
    copies = []
    for k, piece in enumerate(pieces):
        rows = pl.multiple_of(lax.rem(at_ref[2] + 4 - k, 4) * HALF, HALF)
        copies.append(pltpu.make_async_copy(piece, target.at[pl.ds(rows, HALF), :], sems.at[k, 0]))
        copies[k].start()
    for copy in copies:
        copy.wait()


def norm_kernel(flow, at_ref, inner_ref, gate_ref, enter_ref, c_ref, row_ref, gain_ref, rows_ref, *refs):
    pieces, refs = refs[:8], refs[8:]
    gate_out, grad_out, send_ref, rate_out, own_ref, other_ref = refs[:6]
    y_ref, sig_ref, normed_out, gain_out, gn_ref, weight_ref, sems = refs[6:]
    x, core = at_ref[0], at_ref[1]
    copies = [pltpu.make_async_copy(pieces[k], weight_ref.at[k], sems.at[k]) for k in range(8)]
    for copy in copies:
        copy.start()
    flow.arrive()
    c = c_ref[...]

    def first(h, squares):
        flow.arrive(h)
        cols = lane(h, 2 * W)
        keep = pair_starts(row_ref, h)
        y = inner_ref[:, cols].astype(F32) + keep * dot(c, pair_state(enter_ref, h))
        gate = gate_ref[:, cols].astype(F32)
        sig = 0.5 * jnp.tanh(0.5 * gate) + 0.5
        u = y * (gate * sig)
        y_ref[:, cols] = y
        sig_ref[:, cols] = sig
        squared = u * u
        return squares + squared[:, :W] + squared[:, W:]

    def second(h, mixed):
        cols = lane(h, 2 * W)
        other = jnp.abs(lax.rem(h, 2) - core)
        slot = 4 * other + lax.rem(x + 4 - lax.div(h, 2), 4)
        gn = dot(rows_ref[...], weight_ref[slot], 1, 1)
        gn_ref[:, cols] = gn
        u = y_ref[:, cols] * (gate_ref[:, cols].astype(F32) * sig_ref[:, cols])
        both = gain_ref[:, cols] * gn * u
        return mixed + both[:, :W] + both[:, W:]

    zero = jnp.zeros((T, W), F32)
    squares = lax.fori_loop(0, H // 2, first, zero)
    for copy in copies:
        copy.wait()
    mixed = lax.fori_loop(0, H // 2, second, zero)
    rstd = lax.rsqrt(row_sum(squares) / INNER + 1e-5)
    pull = rstd * rstd * rstd * (row_sum(mixed) / INNER)
    rate_out[...] = zero

    @pl.loop(0, H // 2)
    def _(h):
        cols = lane(h, 2 * W)
        y, sig, gn = y_ref[:, cols], sig_ref[:, cols], gn_ref[:, cols]
        gain = gain_ref[:, cols]
        gate = gate_ref[:, cols].astype(F32)
        active = gate * sig
        u = y * active
        normal = u * rstd
        grad_u = rstd * (gain * gn) - u * pull
        grad_y = grad_u * active
        gate_out[:, cols] = (grad_u * y * (sig + active * (1.0 - sig))).astype(BF16)
        normed_out[:, cols] = (normal * gain).astype(BF16)
        gain_out[:, cols] = jnp.sum(gn * normal, axis=0, keepdims=True)
        grad_out[:, cols] = grad_y.astype(BF16)
        start = (grad_y * pair_starts(row_ref, h)).astype(BF16)
        rate = grad_y * y
        at = iota((T, W), 1)
        rates = rate_out[...]
        rates = jnp.where(at == 2 * h, row_sum(rate[:, :W]), rates)
        rate_out[...] = jnp.where(at == 2 * h + 1, row_sum(rate[:, W:]), rates)
        split_state(send_ref, h, dot(c, start, 0, 0).astype(BF16))
        flow.leave(h)

    flow.leave()
    normed = normed_out[...]
    for at, out, target in ((5, other_ref, 1 - core), (4, own_ref, core)):
        for k in range(4):
            block = lax.rem(x + k, 4) * 2 + target
            out[k, 0:W, :] = dot(rows_ref[:, lane(block)], normed, 0, 0).astype(BF16)
            gain = jnp.broadcast_to(gain_out[:, lane(block, 2 * W)], (GAINROWS, 2 * W))
            out[k, W : W + GAINROWS, :] = jnp.zeros((GAINROWS, INNER), BF16)
            out[k, W : W + GAINROWS, 0 : 2 * W] = gain.astype(BF16)
            flow.outgoing.copy(at, k).start()


def opposite_kernel(flow, own_far, other_far, forth_ref, back_ref, own_term, other_term, sems):
    pairs = ((own_far, own_term), (other_far, other_term))
    copies = [pltpu.make_async_copy(far.at[2], near, sems.at[k]) for k, (far, near) in enumerate(pairs)]
    for copy in copies:
        copy.start()
    for copy in copies:
        copy.wait()
    total = (own_term[...].astype(F32) + other_term[...].astype(F32)).astype(BF16)
    forth_ref[...] = total[:, :D]
    back_ref[...] = total[:, D:]
    flow.leave()


def add_kernel(flow, own_term, other_term, *outs):
    for at, k in enumerate((0, 1, 3)):
        flow.arrive(k * STEP)
        outs[at][...] = (own_term[k].astype(F32) + other_term[k].astype(F32)).astype(BF16)
        flow.outgoing.copy(at).start()
    flow.arrive(2 * STEP)


def relay_kernel(flow, right_in, left_in, forth_in, back_in, right_ref, left_ref):
    flow.arrive()
    right_ref[:, :D] = (right_in[:, :D].astype(F32) + forth_in[...].astype(F32)).astype(BF16)
    right_ref[:, D:] = right_in[:, D:]
    left_ref[:, :D] = left_in[:, :D]
    left_ref[:, D:] = (left_in[:, D:].astype(F32) + back_in[...].astype(F32)).astype(BF16)
    flow.leave()


def pair_kernel(
    flow, x_ref, grad_ref, b_ref, c_ref, row_ref, enter_ref,
    inner_ref, grad_c_ref, grad_b_ref, sum_ref,
):
    flow.arrive()
    b, c = b_ref[...], c_ref[...]
    scores = dot(b, c, 1, 1)
    causal = iota((T, T), 0) <= iota((T, T), 1)
    sum_ref[...] = jnp.zeros((T, T), F32)

    def step(pair, total):
        flow.arrive(pair)
        weights = []
        for h in (2 * pair, 2 * pair + 1):
            col = column(row_of(row_ref, h))
            differ = row_of(row_ref, h) - jnp.concatenate([col, col], axis=1)
            table = jnp.exp(jnp.where(causal, differ, FAR))
            grad = grad_ref[:, lane(h)]
            inner_ref[:, lane(h)] = dot((scores * table).astype(BF16), grad)
            weights.append(dot(x_ref[:, lane(h)], grad, 1, 1) * table)
        sum_ref[...] += weights[0] + weights[1]
        flow.leave(pair)
        start = (grad_ref[:, lane(pair, 2 * W)].astype(F32) * pair_starts(row_ref, pair)).astype(BF16)
        return total + dot(start, pair_state(enter_ref, pair), 1, 1)

    carried = lax.fori_loop(0, PAIRS, step, jnp.zeros((T, W), F32))
    weights = sum_ref[...].astype(BF16)
    grad_b_ref[...] = dot(weights, c)
    grad_c_ref[...] = (carried + dot(weights, b, 0, 0)).astype(BF16)
    flow.leave()


def sum_kernel(flow, *refs):
    *terms, out_ref, gain_ref = refs
    flow.arrive()
    total = terms[0][...].astype(F32)
    for term in terms[1:]:
        total = total + term[...].astype(F32)
    out_ref[...] = total[0:W, :].astype(BF16)
    gain_ref[...] = total[W : W + 8, 0 : 2 * W]
    flow.leave()


def last_kernel(
    flow, inner_ref, leave_ref, b_ref, x_ref, row_ref, grad_b_in, rate_ref, state_ref, enter_ref,
    grad_x_ref, grad_b_ref, decay_ref,
):
    flow.arrive()
    b = b_ref[...]

    def step(h, carry):
        flow.arrive(h)
        grad_b, rates, tail = carry
        cols = lane(h, 2 * W)
        leave = pair_state(leave_ref, h)
        keep, total = pair_ends(row_ref, h)
        grad_x = inner_ref[:, cols] + keep * dot(b, leave)
        grad_x_ref[:, cols] = grad_x.astype(BF16)
        flow.leave(h)
        x = x_ref[:, cols].astype(F32)
        rate = x * grad_x
        at = iota((T, W), 1)
        rates = rates - jnp.where(at == 2 * h, row_sum(rate[:, :W]), 0.0)
        rates = rates - jnp.where(at == 2 * h + 1, row_sum(rate[:, W:]), 0.0)
        state = pair_state(state_ref, h).astype(F32)
        later = jnp.exp(total) * pair_state(enter_ref, h).astype(F32) + state
        across = jnp.sum(later * leave.astype(F32), axis=0, keepdims=True)
        at = iota((W, 1), 0)
        tail = tail + jnp.where(at == 2 * h, row_sum(across[:, :W]), 0.0)
        tail = tail + jnp.where(at == 2 * h + 1, row_sum(across[:, W:]), 0.0)
        return grad_b + dot((x * keep).astype(BF16), leave, 1, 1), rates, tail

    start = (grad_b_in[...], rate_ref[...], jnp.zeros((W, 1), F32))
    grad_b, rates, tail = lax.fori_loop(0, H // 2, step, start)
    grad_b_ref[...] = grad_b.astype(BF16)
    lower = (iota((T, T), 0) >= iota((T, T), 1)).astype(F32)
    decay_ref[...] = (dot(rates, lower, 0, 0, precision=HI) + tail)[:H, :]
    flow.leave()


PAIRS = H // 2
CHUNKS = 4
STEP = PAIRS // CHUNKS


def chunked(array):
    return array.shape == (T, INNER) or len(array.shape) == 3 and array.shape[0] in (4, SEQ)


def part(ref, h):
    if len(ref.shape) == 2:
        return ref.at[:, lane(h, 2 * W * STEP)]
    count = ref.shape[0] // CHUNKS
    return ref.at[pl.ds(h * count, count)]


class Traffic:
    def __init__(self, sources, targets, sems):
        self.pairs = list(zip(sources, targets, range(len(sources))))
        self.sems = sems

    def copy(self, k, h=None):
        source, target, at = self.pairs[k]
        if h is None:
            return pltpu.make_async_copy(source, target, self.sems.at[at, 0])
        return pltpu.make_async_copy(part(source, h), part(target, h), self.sems.at[at, h])

    def where(self, pieces):
        return [k for k, (source, _, _) in enumerate(self.pairs) if chunked(source) == pieces]


class Flow:
    def __init__(self, incoming, outgoing):
        self.incoming, self.outgoing = incoming, outgoing

    def begin(self):
        for k in self.incoming.where(False):
            self.incoming.copy(k).start()
        for h in range(CHUNKS):
            for k in self.incoming.where(True):
                self.incoming.copy(k, h).start()

    def arrive(self, pair=None, last_first=False):
        if pair is None:
            for k in self.incoming.where(False):
                self.incoming.copy(k).wait()
            return

        @pl.when(lax.rem(pair, STEP) == (STEP - 1 if last_first else 0))
        def _():
            for k in self.incoming.where(True):
                self.incoming.copy(k, lax.div(pair, STEP)).wait()

    def leave(self, pair=None, last_first=False):
        if pair is None:
            for k in self.outgoing.where(False):
                self.outgoing.copy(k).start()
            return

        @pl.when(lax.rem(pair, STEP) == (0 if last_first else STEP - 1))
        def _():
            for k in self.outgoing.where(True):
                if self.outgoing.pairs[k][0].shape[0] != 4:
                    self.outgoing.copy(k, lax.div(pair, STEP)).start()

    def end(self):
        for k in self.outgoing.where(False):
            self.outgoing.copy(k).wait()
        for h in range(CHUNKS):
            for k in self.outgoing.where(True):
                self.outgoing.copy(k, h).wait()


def call(kernel, outs, args, scratch=(), smem=0, us=1.0, loose=(), after=(), own=False, near=(), raw=()):
    scalars, arrays = args[:smem], args[smem:]
    held = sum(a.size * a.dtype.itemsize for a in (*arrays, *outs))
    room = held + sum(math.prod(s.shape) * 4 for s in scratch)
    spaces = [next((space for group, space in ((near, pltpu.VMEM), (loose, pl.ANY)) if any(a is b for b in group)), pltpu.HBM) for a in arrays]
    direct = [space is pltpu.VMEM or any(a is b for b in raw) for a, space in zip(arrays, spaces)]
    kept = [] if own else [a for a, skip in zip(arrays, direct) if not skip]
    counts = (smem, len(arrays), len(after), len(outs), len(kept), len(outs), len(scratch))

    def run(*refs):
        groups = []
        for count in counts:
            groups.append(refs[:count])
            refs = refs[count:]
        numbers, sources, _, targets, copies, near_out, rest = groups
        far = [source for source, skip in zip(sources, direct) if not skip]
        flow = Flow(Traffic(far, copies, refs[0]), Traffic(near_out, targets, refs[1]))
        if own:
            kernel(flow, *numbers, *sources, *near_out, *rest, refs[0])
        else:
            flow.begin()
            copies = list(copies)
            near_in = [source if skip else copies.pop(0) for source, skip in zip(sources, direct)]
            kernel(flow, *numbers, *near_in, *near_out, *rest)
        flow.end()

    def tie(array, space):
        return array if space is pl.ANY else pltpu.with_memory_space_constraint(array, space)

    tied = [tie(a, space) for a, space in zip(arrays, spaces)]
    return pl.pallas_call(
        run,
        out_shape=[pltpu.HBM(out.shape, out.dtype) for out in outs],
        in_specs=[pl.BlockSpec(memory_space=pltpu.SMEM)] * smem
        + [pl.BlockSpec(memory_space=space) for space in spaces]
        + [pl.BlockSpec(memory_space=pl.ANY)] * len(after),
        out_specs=[pl.BlockSpec(memory_space=pltpu.HBM)] * len(outs),
        scratch_shapes=[
            *(pltpu.VMEM(a.shape, a.dtype) for a in (*kept, *outs)),
            *scratch,
            pltpu.SemaphoreType.DMA((len(arrays), CHUNKS)),
            pltpu.SemaphoreType.DMA((len(outs), CHUNKS)),
        ],
        compiler_params=pltpu.CompilerParams(vmem_limit_bytes=room + 6 * 2**20),
        cost_estimate=pl.CostEstimate(flops=int(us * 1.1e9), bytes_accessed=held, transcendentals=0),
    )(*scalars, *tied, *(pltpu.with_memory_space_constraint(a, pltpu.HBM) for a in after))


def shaped(shape, dtype=F32):
    return jax.ShapeDtypeStruct(shape, dtype)


def shift(value, axis, by):
    size = lax.axis_size(axis)
    return lax.ppermute(value, axis, [(i, (i + by) % size) for i in range(size)])


def shifts(values, axis):
    return [value if k == 0 else shift(value, axis, k) for k, value in enumerate(values)]


def exchange(value, axes=SEQ_AXES):
    return lax.all_to_all(value, axes, 0, 0, tiled=True)


def body(ssm, gate, state_in, state_out, log_decay, gain, out_weight, grad_rows):
    x, b, c = ssm[0], state_in[0], state_out[0]
    gate, grad_rows, gain_row = gate[0], grad_rows[0], gain[None]
    at = jnp.stack([lax.axis_index(name) for name in ("x", "c", "y")]).astype(jnp.int32)
    wide = shaped((T, INNER))
    wide_bf = shaped((T, INNER), BF16)
    states = shaped((SEQ, HALF, W), BF16)

    send, row = call(
        state_kernel,
        [shaped((SEQ, HALF + EXTRA, W), BF16), shaped((H, T))],
        [x, b, log_decay[0].T],
        us=0.1,
    )
    got = exchange(send)

    own = exchange(jnp.broadcast_to(out_weight.T, (8, 8, D)), "z").reshape(HALF, D)
    [inner] = call(inner_kernel, [wide_bf], [x, b, c, row], us=0.3)
    slices = shifts([own] * 4, "y")
    [ordered] = call(
        order_kernel, [shaped((T, D), BF16)], [at, *slices], smem=1, us=0.1, loose=slices, own=True, after=[inner]
    )
    pieces = shifts([ordered] * 4, "x")
    pieces += [shift(piece, "c", 1) for piece in pieces]

    enter_part, factor = call(
        forward_scan_kernel, [states, shaped((SEQ, W))], [got], us=0.1, loose=[got]
    )
    enter = exchange(enter_part)
    grad_gate, grad_y, grad_send, rate, own_term, other_term = call(
        norm_kernel,
        [wide_bf, wide_bf, states, shaped((T, W)), *[shaped((4, W + GAINROWS, INNER), BF16)] * 2],
        [at, inner, gate, enter, c, row, gain_row, grad_rows, *pieces],
        scratch=[
            pltpu.VMEM((T, INNER), F32),
            pltpu.VMEM((T, INNER), F32),
            pltpu.VMEM((T, INNER), BF16),
            pltpu.VMEM((1, INNER), F32),
            pltpu.VMEM((T, INNER), F32),
            pltpu.VMEM((8, T, D), BF16),
            pltpu.SemaphoreType.DMA((8,)),
        ],
        smem=1,
        us=1.3,
        loose=[enter, *pieces[1:5], pieces[7]],
        raw=pieces,
    )
    grad_got = exchange(grad_send)
    other_term = shift(other_term, "c", 1)
    block = shaped((W + GAINROWS, INNER), BF16)
    half = shaped((W + GAINROWS, D), BF16)
    forth, back = call(
        opposite_kernel,
        [half, half],
        [own_term, other_term],
        scratch=[
            pltpu.VMEM((W + GAINROWS, INNER), BF16),
            pltpu.VMEM((W + GAINROWS, INNER), BF16),
            pltpu.SemaphoreType.DMA((2,)),
        ],
        us=1.2,
        loose=[other_term],
        raw=[own_term, other_term],
    )
    kept, right, left = call(
        add_kernel, [block] * 3, [own_term, other_term], us=2.5, loose=[other_term], after=[forth]
    )
    forth, back = shift(forth, "x", 1), shift(back, "x", -1)
    right, left = call(
        relay_kernel, [block, block], [right, left, forth, back], us=2.8, near=[forth, back]
    )
    [leave_part] = call(
        backward_scan_kernel, [states], [grad_got, factor], us=2.0, loose=[grad_got], after=[right]
    )
    leave = exchange(leave_part)
    right, left = shift(right, "x", 1), shift(left, "x", -1)
    quarter, gains = call(
        sum_kernel,
        [shaped((W, INNER), BF16), shaped((8, 2 * W))],
        [kept, right, left],
        us=2.6,
        near=[right, left],
    )
    grad_inner, grad_state_out, grad_b = call(
        pair_kernel,
        [wide, shaped((T, W), BF16), shaped((T, W))],
        [x, grad_y, b, c, row, enter],
        scratch=[pltpu.VMEM((T, T), F32)],
        us=5.8,
        loose=[enter],
        after=[leave_part],
    )
    rows = quarter.reshape(SEQ, HALF, W)
    gains = jnp.pad(gains[0].astype(BF16).reshape(SEQ, 1, 8), ((0, 0), (0, 7), (0, W - 8)))
    final = jnp.sum(exchange(jnp.concatenate([rows, gains], axis=1)).astype(F32), axis=0)
    grad_input, grad_state_in, grad_log_decay = call(
        last_kernel,
        [wide_bf, shaped((T, W), BF16), shaped((H, T))],
        [grad_inner, leave, b, x, row, grad_b, rate, send, enter],
        us=5.5,
        loose=[leave, enter],
    )
    return (
        grad_input[None],
        grad_gate[None],
        grad_state_in[None],
        grad_state_out[None],
        grad_log_decay.T[None],
        final[:HALF].reshape(4, INNER),
        final[HALF, :8],
    )


def solution(mesh):
    split = Mesh(mesh.devices.reshape(4, 2, 4, 8), ("x", "c", "y", "z"))
    shower, seq = ("x", "c"), ("y", "z")
    rows = P(shower, seq, None)
    every = (*shower, *seq)
    return jax.shard_map(
        body,
        mesh=split,
        in_specs=(rows, rows, rows, rows, rows, P(), P(None, every), rows),
        out_specs=(rows, rows, rows, rows, rows, P(every, None), P(every)),
        check_vma=False,
    )
```
